32 devices in a mesh: group: 4 (over y, x), member: 2 (over core), space: 4 (over z).
Axes of the slice: x: 2, y: 2, z: 4, core: 2. Of those that a mesh axis runs over, the one named last changes fastest.
Arguments:
- height_velocity_tensor: float32 [256, 3, 128, 128], P(('group', 'member'), None, 'space'), may hold values from -6 to 6
- obs_values: float32 [32, 768], P(('group', 'member', 'space')), may hold values from -6 to 6
- obs_precision: float32 [32, 768], P(('group', 'member', 'space')), may hold values from 0.3 to 3
- obs_index: int32 [32, 768], P(('group', 'member', 'space')), may hold values from 0 to 1535, as said below
Outputs:
- analysis: float32 [256, 3, 128, 128], P(('group', 'member'), None, 'space')
The draws below stay inside these ranges and needn't reach their ends.
Inputs may be any that keep to these rules, and one draw needn't show every extreme that they name: `obs_index`: each row holds 768 distinct positions among the 1536 values of its block.
All inputs are finite; a program needn't handle non-finite values.
Results may differ from the reference program's by a relative error of at most 0.00013.
Values sent between devices are 32-bit elements; how exact they have to be, the bound alone decides.
No kernel may reach another device: no remote copies, remote signals or barrier semaphores. Data moves between devices by JAX's collectives and lax.ppermute only.
A program may use at most 64 MiB of HBM per device.

```python
import math
import jax
import jax.numpy as jnp
from jax import lax

TRAJECTORY_COUNT = 256
CX = 32
NY = 128
STEPS = 2
NX = 128
TILE_POINTS = 512
OBS_BLK = 768
BLOCKS = 32
N_GROUP = 4
N_MEMBER = 2
N_SPACE = 4


def draw_obs_index(key, part):
    keys = jax.random.split(jax.random.fold_in(key, 17), BLOCKS)

    def one_row(row_key):
        shuffled = jax.random.permutation(row_key, 3 * TILE_POINTS - 2) + 1
        picked = shuffled[:OBS_BLK - 2].astype(jnp.int32)
        first = jnp.zeros((1,), jnp.int32)
        last = jnp.full((1,), 3 * TILE_POINTS - 1, jnp.int32)
        return jnp.concatenate([first, last, picked])
    return jax.vmap(one_row)(keys)


def levels(own_key, dims, shards, least, top_value):
    gain = 1.0
    for axis_at, parts in shards:
        draws = jax.random.uniform(jax.random.fold_in(jax.random.fold_in(own_key, 6), axis_at), (parts,), jnp.float32, least / len(shards), top_value / len(shards))
        gain = gain * jnp.repeat(jnp.exp(draws), dims[axis_at] // parts).reshape((-1,) + (1,) * (len(dims) - 1 - axis_at))
    return gain


def scatter_about(stream_key, dims, scale, reach, cuts=(), kind=jnp.bfloat16):
    entries = jax.random.normal(stream_key, dims, jnp.float32) * scale
    if len(cuts) > 0:
        entries = levels(stream_key, dims, cuts, -0.22, 0.18) * entries
    return jnp.clip(entries, min=-reach, max=reach).astype(kind)


def setup_inputs(seed: int = 0) -> dict:
    streams_of = jax.random.split(jax.random.key(seed), 5)
    height_velocity_tensor = scatter_about(streams_of[0], (TRAJECTORY_COUNT, 3, NX, NY), 1.0, 6.0, ((0, 8), (2, 4)), jnp.float32)
    obs_values = scatter_about(streams_of[1], (BLOCKS, OBS_BLK), 1.0, 6.0, ((0, 32),), jnp.float32)
    obs_precision = jnp.clip(jnp.exp(math.log(3.0) - 2.3025851 * jax.random.uniform(streams_of[2], (BLOCKS, OBS_BLK), jnp.float32) ** levels(streams_of[2], (BLOCKS, OBS_BLK), ((0, 32),), -0.2, 0.2)), 0.3, 3.0)
    obs_index = draw_obs_index(jax.random.fold_in(streams_of[4], 71), 0)
    return {"height_velocity_tensor": height_velocity_tensor, "obs_values": obs_values, "obs_precision": obs_precision, "obs_index": obs_index}


grav_coef = 0.4
depth_coef = 0.4

def across_y(field):
    return jnp.roll(field, -1, axis=-1) - jnp.roll(field, 1, axis=-1)

def across_x(field):
    padded = jnp.pad(field, ((1, 1), (0, 0)))
    return padded[2:] - padded[:-2]

def trajectory_prediction(layered_quantities):
    height, flow_x, flow_y = (layered_quantities[0], layered_quantities[1], layered_quantities[2])
    for stepped in range(STEPS):
        new_x = flow_x - grav_coef * across_x(height)
        new_y = flow_y - grav_coef * across_y(height)
        height = height - depth_coef * (across_x(new_x) + across_y(new_y))
        flow_x, flow_y = (new_x, new_y)
    return jnp.stack([height, flow_x, flow_y])

def take_values(values, picks):
    return jnp.take(values, picks, axis=-1)

def make_transform(gram, pull):
    identity = jnp.eye(gram.shape[0], dtype=jnp.float32)
    factor = jnp.linalg.cholesky(identity + gram)
    inverse = jax.scipy.linalg.solve_triangular(factor, identity, lower=True)
    inner = jnp.dot(inverse, pull, precision=lax.Precision.HIGHEST)
    weights_mean = jnp.dot(inverse.T, inner, precision=lax.Precision.HIGHEST)
    return inverse + weights_mean[None, :]

def reference(height_velocity_tensor, obs_values, obs_precision, obs_index):
    predicted_model_vector = lax.map(trajectory_prediction, height_velocity_tensor)
    trajectory_clusters = N_GROUP * N_MEMBER
    tile_partition = predicted_model_vector.reshape(TRAJECTORY_COUNT, 3, N_SPACE, trajectory_clusters, TILE_POINTS)
    ens_mean = lax.optimization_barrier(jnp.mean(tile_partition, axis=0))
    anomaly = tile_partition - ens_mean
    anomaly_blocks = jnp.transpose(anomaly, (3, 2, 0, 1, 4)).reshape(trajectory_clusters, N_SPACE, TRAJECTORY_COUNT, 3 * TILE_POINTS)
    mean_blocks = jnp.transpose(ens_mean, (2, 1, 0, 3)).reshape(trajectory_clusters, N_SPACE, 3 * TILE_POINTS)
    picks = obs_index.reshape(trajectory_clusters, N_SPACE, OBS_BLK)
    seen = jax.vmap(jax.vmap(take_values))(anomaly_blocks, picks)
    seen_mean = jax.vmap(jax.vmap(take_values))(mean_blocks, picks)
    precision = obs_precision.reshape(trajectory_clusters, N_SPACE, OBS_BLK)
    observed = obs_values.reshape(trajectory_clusters, N_SPACE, OBS_BLK)
    scale = 1.0 / math.sqrt(TRAJECTORY_COUNT - 1)
    scaled = seen * precision[:, :, None, :] * scale
    innovation = precision * (observed - seen_mean) * scale
    columns = jnp.transpose(scaled, (2, 0, 1, 3)).reshape(TRAJECTORY_COUNT, -1)
    gram = jnp.dot(columns, columns.T, precision=lax.Precision.HIGHEST)
    pull = jnp.dot(columns, innovation.reshape(-1), precision=lax.Precision.HIGHEST)
    transform = make_transform(gram, pull)
    update = jnp.dot(transform, anomaly.reshape(TRAJECTORY_COUNT, -1), precision=lax.Precision.HIGHEST)
    result = ens_mean.reshape(1, -1) + update
    return result.reshape(TRAJECTORY_COUNT, 3, N_SPACE * CX, NY)
```

```python
import functools
import math

import jax
import jax.numpy as jnp
from jax import lax
from jax.experimental import pallas as pl
from jax.experimental.pallas import tpu as pltpu
from jax.sharding import PartitionSpec as P

STEPS = 2
GRAV = 0.4
DEPTH = 0.4
HALO = (4, 3, 2)
HALO_ROWS = sum(HALO)
LANES = 128
VMEM_LIMIT = 40 * 1024 * 1024


def whole(shape, memory_space=pltpu.VMEM):
    return pl.BlockSpec(memory_space=memory_space)


def call(kernel, out_shape, n_in, scratch=(), **kw):
    single = not isinstance(out_shape, (list, tuple))
    n_out = 1 if single else len(out_shape)
    spec = pl.BlockSpec(memory_space=pltpu.VMEM)
    return pl.pallas_call(
        kernel,
        out_shape=out_shape,
        in_specs=[spec] * n_in,
        out_specs=spec if single else [spec] * n_out,
        scratch_shapes=list(scratch),
        compiler_params=pltpu.CompilerParams(vmem_limit_bytes=VMEM_LIMIT),
        **kw,
    )


def f32(*shape):
    return jax.ShapeDtypeStruct(shape, jnp.float32)


def pack_kernel(top_ref, bottom_ref, to_prev_ref, to_next_ref):
    fields, edge = top_ref.shape[1], top_ref.shape[2]
    at = 0
    for field, rows in enumerate(HALO):
        for row in range(rows):
            to_prev_ref[at] = top_ref[:, field, row, :]
            to_next_ref[at] = bottom_ref[:, field, edge - rows + row, :]
            at += 1


def pack_edges(state):
    members, fields, rows, cols = state.shape
    edge = 8
    last = rows // edge - 1
    block = (members, fields, edge, cols)
    out = f32(HALO_ROWS, members, cols)
    out_spec = pl.BlockSpec((HALO_ROWS, members, cols), lambda i: (0, 0, 0))
    return pl.pallas_call(
        pack_kernel,
        grid=(1,),
        out_shape=[out, out],
        in_specs=[
            pl.BlockSpec(block, lambda i: (0, 0, 0, 0)),
            pl.BlockSpec(block, lambda i: (0, 0, last, 0)),
        ],
        out_specs=[out_spec, out_spec],
        compiler_params=pltpu.CompilerParams(vmem_limit_bytes=VMEM_LIMIT),
    )(state, state)


def forecast_kernel(dims, state_ref, before_ref, after_ref, out_ref):
    members, fields, rows, cols, block_rows = dims
    here = lax.axis_index("space")
    has_before = (here > 0).astype(jnp.float32)
    has_after = (here < lax.axis_size("space") - 1).astype(jnp.float32)

    def across_y(value):
        return pltpu.roll(value, cols - 1, 1) - pltpu.roll(value, 1, 1)

    def inside(value, row):
        if row < 0:
            return value * has_before
        if row >= rows:
            return value * has_after
        return value

    for first in range(0, members, 8):

        def load(field, row):
            offset = sum(HALO[:field])
            if row < 0:
                return before_ref[offset + HALO[field] + row, first : first + 8, :]
            if row >= rows:
                return after_ref[offset + row - rows, first : first + 8, :]
            start = (first * fields + field) * rows + row
            return state_ref[pl.ds(start, 8, stride=fields * rows), :]

        height, flow_x, flow_y = {}, {}, {}
        height_1, flow_x1, flow_y1 = {}, {}, {}
        flow_x2, flow_y2 = {}, {}

        def store(field, row, value):
            out_ref[row // block_rows, field * block_rows + row % block_rows, first : first + 8, :] = value

        height[-4] = load(0, -4)
        height[-3] = load(0, -3)
        for lead in range(-3, rows + 7):
            row = lead
            if row < rows + 3:
                height[row + 1] = load(0, row + 1)
                flow_x1[row] = inside(
                    load(1, row) - GRAV * (height[row + 1] - height[row - 1]), row
                )
                if -2 <= row < rows + 2:
                    flow_y1[row] = load(2, row) - GRAV * across_y(height[row])
            row = lead - 1
            if -2 <= row < rows + 2:
                height_1[row] = inside(
                    height[row]
                    - DEPTH * (flow_x1[row + 1] - flow_x1[row - 1] + across_y(flow_y1[row])),
                    row,
                )
            row = lead - 2
            if -1 <= row < rows + 1:
                flow_x2[row] = inside(
                    flow_x1[row] - GRAV * (height_1[row + 1] - height_1[row - 1]), row
                )
                if 0 <= row < rows:
                    flow_y2[row] = flow_y1[row] - GRAV * across_y(height_1[row])
                    store(1, row, flow_x2[row])
                    store(2, row, flow_y2[row])
            row = lead - 3
            if 0 <= row < rows:
                store(
                    0,
                    row,
                    height_1[row]
                    - DEPTH * (flow_x2[row + 1] - flow_x2[row - 1] + across_y(flow_y2[row])),
                )


def forecast(state, clusters):
    members, fields, rows, cols = state.shape
    block_rows = rows // clusters
    to_prev, to_next = pack_edges(state)
    count = lax.axis_size("space")
    before = lax.ppermute(to_next, "space", [(i, i + 1) for i in range(count - 1)])
    after = lax.ppermute(to_prev, "space", [(i + 1, i) for i in range(count - 1)])
    dims = (members, fields, rows, cols, block_rows)
    return call(
        functools.partial(forecast_kernel, dims),
        f32(clusters, fields * block_rows, members, cols),
        3,
    )(state.reshape(members * fields * rows, cols), before, after)


def split(value):
    high = value.astype(jnp.bfloat16)
    rest = value - high.astype(jnp.float32)
    middle = rest.astype(jnp.bfloat16)
    low = (rest - middle.astype(jnp.float32)).astype(jnp.bfloat16)
    return high, middle, low


def observed_kernel(values_ref, precision_ref, index_ref, out_ref):
    count = index_ref.shape[1]
    width = out_ref.shape[1]
    parts = list(split(precision_ref[...])) + list(split(values_ref[...]))
    pad = jnp.zeros((16 - len(parts), count), jnp.bfloat16)
    rows = jnp.concatenate(parts + [pad], axis=0)
    position = lax.broadcasted_iota(jnp.int32, (width, count), 0)
    hit = (position == index_ref[...]).astype(jnp.float32).astype(jnp.bfloat16)
    placed = lax.dot_general(
        rows, hit, (((1,), (1,)), ((), ())), preferred_element_type=jnp.float32
    )
    out_ref[0:1, :] = placed[0:1] + placed[1:2] + placed[2:3]
    out_ref[1:2, :] = placed[3:4] + placed[4:5] + placed[5:6]
    out_ref[2:8, :] = jnp.zeros((6, width), jnp.float32)


def gram_kernel(dims, forecast_ref, observed_ref, out_ref, scaled_ref):
    clusters, terms, members, cols = dims
    total = clusters * members
    scale = 1.0 / math.sqrt(total - 1)
    half = LANES
    for term in range(terms):
        at = slice(term * cols, (term + 1) * cols)
        values = forecast_ref[:, term].reshape(total, cols)
        mean = jnp.sum(values, axis=0, keepdims=True) * (1.0 / total)
        weight = observed_ref[0:1, at] * scale
        scaled_ref[0:total, at] = (values - mean) * weight
        innovation = (observed_ref[1:2, at] - mean) * weight
        scaled_ref[total : total + 8, at] = jnp.concatenate(
            [innovation, jnp.zeros((7, cols), jnp.float32)], axis=0
        )
    product = lax.dot_general(
        scaled_ref[...],
        scaled_ref[0:total, :],
        (((1,), (1,)), ((), ())),
        precision=lax.Precision.HIGHEST,
        preferred_element_type=jnp.float32,
    )
    at = 0
    for first in range(0, total, half):
        out_ref[at : at + total - first, :] = product[first:total, first : first + half]
        at += total - first
    for k, first in enumerate(range(0, total, half)):
        out_ref[at + 8 * k : at + 8 * k + 8, :] = product[total : total + 8, first : first + half]
    at += 8 * (total // half)
    if at < out_ref.shape[0]:
        out_ref[at:, :] = jnp.zeros((out_ref.shape[0] - at, half), jnp.float32)


def flip(value, axis, bits):
    return lax.ppermute(value, axis, [(i, i ^ bits) for i in range(lax.axis_size(axis))])


def total_over_devices(value):
    sizes = tuple(lax.axis_size(axis) for axis in ("group", "member", "space"))
    if sizes != (4, 2, 4):
        return lax.psum(value, ("group", "member", "space"))
    rows, cols = value.shape
    core = lax.axis_index("member")
    chip = lax.axis_index("group")
    half = rows // 2
    part = half // 4
    kept = lax.dynamic_slice_in_dim(value, core * half, half, 0)
    given = lax.dynamic_slice_in_dim(value, (1 - core) * half, half, 0)
    summed = (kept + flip(given, "member", 1)).reshape(4, part, cols)
    pieces = [lax.dynamic_index_in_dim(summed, chip ^ s, 0, False) for s in range(4)]
    piece = pieces[0] + (
        flip(pieces[1], "group", 1) + flip(pieces[2], "group", 2) + flip(pieces[3], "group", 3)
    )
    piece = piece + (flip(piece, "space", 1) + flip(piece, "space", 2) + flip(piece, "space", 3))
    got = jnp.stack([piece] + [flip(piece, "group", s) for s in (1, 2, 3)], axis=0)
    mine = jnp.concatenate(
        [lax.dynamic_index_in_dim(got, chip ^ i, 0, False) for i in range(4)], axis=0
    )
    other = flip(mine, "member", 1)
    return jnp.concatenate(
        [jnp.where(core == 0, mine, other), jnp.where(core == 0, other, mine)], axis=0
    )


def make_transform(packed, total):
    half = LANES
    columns = []
    at = 0
    for first in range(0, total, half):
        column = packed[at : at + total - first]
        columns.append(jnp.pad(column, ((first, 0), (0, 0))))
        at += total - first
    gram = jnp.concatenate(columns, axis=1)
    pull = jnp.concatenate([packed[at + 8 * k] for k in range(total // half)])
    identity = jnp.eye(total, dtype=jnp.float32)
    factor = lax.linalg.cholesky(identity + gram, symmetrize_input=False)
    inverse = jax.scipy.linalg.solve_triangular(factor, identity, lower=True)
    inner = jnp.dot(inverse, pull, precision=lax.Precision.HIGHEST)
    weights_mean = jnp.dot(inverse.T, inner, precision=lax.Precision.HIGHEST)
    return inverse + weights_mean[None, :]


def update_kernel(dims, forecast_ref, transform_ref, out_ref):
    clusters, terms, members, cols = dims
    total = clusters * members
    transform = transform_ref[...]
    step = 2
    for first in range(0, terms, step):
        some = range(first, min(first + step, terms))
        values = [forecast_ref[:, term].reshape(total, cols) for term in some]
        means = [jnp.sum(v, axis=0, keepdims=True) * (1.0 / total) for v in values]
        anomaly = jnp.concatenate([v - m for v, m in zip(values, means)], axis=1)
        updated = lax.dot_general(
            transform,
            anomaly,
            (((1,), (0,)), ((), ())),
            precision=lax.Precision.HIGHEST,
            preferred_element_type=jnp.float32,
        ) + jnp.concatenate(means, axis=1)
        for k, term in enumerate(some):
            out_ref[:, term] = updated[:, k * cols : (k + 1) * cols].reshape(clusters, members, cols)


def place_kernel(dims, in_ref, out_ref):
    clusters, fields, block_rows, members, cols = dims
    rows = clusters * block_rows
    for cluster in range(clusters):
        for field in range(fields):
            for row in range(block_rows):
                at = field * rows + cluster * block_rows + row
                out_ref[pl.ds(at, members, stride=fields * rows), :] = in_ref[
                    cluster, field * block_rows + row
                ]


def on_device(state, obs_values, obs_precision, obs_index):
    members, fields, rows, cols = state.shape
    clusters = lax.axis_size("group") * lax.axis_size("member")
    block_rows = rows // clusters
    terms = fields * block_rows
    total = clusters * members
    dims = (clusters, terms, members, cols)
    predicted = forecast(state, clusters)
    arrived = lax.all_to_all(predicted, ("group", "member"), split_axis=0, concat_axis=0, tiled=True)
    observed = call(observed_kernel, f32(8, terms * cols), 3)(obs_values, obs_precision, obs_index)
    packed = call(
        functools.partial(gram_kernel, dims),
        f32(448, LANES),
        2,
        [pltpu.VMEM((total + 8, terms * cols), jnp.float32)],
    )(arrived, observed)
    packed = total_over_devices(packed)
    transform = make_transform(packed, total)
    updated = call(
        functools.partial(update_kernel, dims), f32(clusters, terms, members, cols), 2
    )(arrived, transform)
    returned = lax.all_to_all(updated, ("group", "member"), split_axis=0, concat_axis=0, tiled=True)
    placed = call(
        functools.partial(place_kernel, (clusters, fields, block_rows, members, cols)),
        f32(members * fields * rows, cols),
        1,
    )(returned)
    return placed.reshape(members, fields, rows, cols)


def solution(mesh):
    blocks = P(("group", "member", "space"), None)
    state = P(("group", "member"), None, "space", None)
    return jax.shard_map(
        on_device,
        mesh=mesh,
        in_specs=(state, blocks, blocks, blocks),
        out_specs=state,
        check_vma=False,
    )
```

```python
import functools
import math

import jax
import jax.numpy as jnp
from jax import lax
from jax.experimental import pallas as pl
from jax.experimental.pallas import tpu as pltpu
from jax.sharding import PartitionSpec as P

STEPS = 2
GRAV = 0.4
DEPTH = 0.4
HALO = (4, 3, 2)
HALO_ROWS = sum(HALO)
LANES = 128
VMEM_LIMIT = 40 * 1024 * 1024


def whole(shape, memory_space=pltpu.VMEM):
    return pl.BlockSpec(memory_space=memory_space)


def call(kernel, out_shape, n_in, scratch=(), **kw):
    single = not isinstance(out_shape, (list, tuple))
    n_out = 1 if single else len(out_shape)
    spec = pl.BlockSpec(memory_space=pltpu.VMEM)
    return pl.pallas_call(
        kernel,
        out_shape=out_shape,
        in_specs=[spec] * n_in,
        out_specs=spec if single else [spec] * n_out,
        scratch_shapes=list(scratch),
        compiler_params=pltpu.CompilerParams(vmem_limit_bytes=VMEM_LIMIT),
        **kw,
    )


def f32(*shape):
    return jax.ShapeDtypeStruct(shape, jnp.float32)


def pack_kernel(top_ref, bottom_ref, to_prev_ref, to_next_ref):
    fields, edge = top_ref.shape[1], top_ref.shape[2]
    at = 0
    for field, rows in enumerate(HALO):
        for row in range(rows):
            to_prev_ref[at] = top_ref[:, field, row, :]
            to_next_ref[at] = bottom_ref[:, field, edge - rows + row, :]
            at += 1


def pack_edges(state):
    members, fields, rows, cols = state.shape
    edge = 8
    last = rows // edge - 1
    block = (members, fields, edge, cols)
    out = f32(HALO_ROWS, members, cols)
    out_spec = pl.BlockSpec((HALO_ROWS, members, cols), lambda i: (0, 0, 0))
    return pl.pallas_call(
        pack_kernel,
        grid=(1,),
        out_shape=[out, out],
        in_specs=[
            pl.BlockSpec(block, lambda i: (0, 0, 0, 0)),
            pl.BlockSpec(block, lambda i: (0, 0, last, 0)),
        ],
        out_specs=[out_spec, out_spec],
        compiler_params=pltpu.CompilerParams(vmem_limit_bytes=VMEM_LIMIT),
    )(state, state)


def forecast_kernel(dims, state_ref, before_ref, after_ref, out_ref):
    members, fields, rows, cols, block_rows = dims
    here = lax.axis_index("space")
    has_before = (here > 0).astype(jnp.float32)
    has_after = (here < lax.axis_size("space") - 1).astype(jnp.float32)

    def across_y(value):
        return pltpu.roll(value, cols - 1, 1) - pltpu.roll(value, 1, 1)

    def inside(value, row):
        if row < 0:
            return value * has_before
        if row >= rows:
            return value * has_after
        return value

    for first in range(0, members, 8):

        def load(field, row):
            offset = sum(HALO[:field])
            if row < 0:
                return before_ref[offset + HALO[field] + row, first : first + 8, :]
            if row >= rows:
                return after_ref[offset + row - rows, first : first + 8, :]
            start = (first * fields + field) * rows + row
            return state_ref[pl.ds(start, 8, stride=fields * rows), :]

        height, flow_x, flow_y = {}, {}, {}
        height_1, flow_x1, flow_y1 = {}, {}, {}
        flow_x2, flow_y2 = {}, {}

        def store(field, row, value):
            out_ref[row // block_rows, field * block_rows + row % block_rows, first : first + 8, :] = value

        height[-4] = load(0, -4)
        height[-3] = load(0, -3)
        for lead in range(-3, rows + 7):
            row = lead
            if row < rows + 3:
                height[row + 1] = load(0, row + 1)
                flow_x1[row] = inside(
                    load(1, row) - GRAV * (height[row + 1] - height[row - 1]), row
                )
                if -2 <= row < rows + 2:
                    flow_y1[row] = load(2, row) - GRAV * across_y(height[row])
            row = lead - 1
            if -2 <= row < rows + 2:
                height_1[row] = inside(
                    height[row]
                    - DEPTH * (flow_x1[row + 1] - flow_x1[row - 1] + across_y(flow_y1[row])),
                    row,
                )
            row = lead - 2
            if -1 <= row < rows + 1:
                flow_x2[row] = inside(
                    flow_x1[row] - GRAV * (height_1[row + 1] - height_1[row - 1]), row
                )
                if 0 <= row < rows:
                    flow_y2[row] = flow_y1[row] - GRAV * across_y(height_1[row])
                    store(1, row, flow_x2[row])
                    store(2, row, flow_y2[row])
            row = lead - 3
            if 0 <= row < rows:
                store(
                    0,
                    row,
                    height_1[row]
                    - DEPTH * (flow_x2[row + 1] - flow_x2[row - 1] + across_y(flow_y2[row])),
                )


def forecast(state, clusters):
    members, fields, rows, cols = state.shape
    block_rows = rows // clusters
    to_prev, to_next = pack_edges(state)
    count = lax.axis_size("space")
    before = lax.ppermute(to_next, "space", [(i, i + 1) for i in range(count - 1)])
    after = lax.ppermute(to_prev, "space", [(i + 1, i) for i in range(count - 1)])
    dims = (members, fields, rows, cols, block_rows)
    return call(
        functools.partial(forecast_kernel, dims),
        f32(clusters, fields * block_rows, members, cols),
        3,
    )(state.reshape(members * fields * rows, cols), before, after)


def split(value):
    high = value.astype(jnp.bfloat16)
    rest = value - high.astype(jnp.float32)
    middle = rest.astype(jnp.bfloat16)
    low = (rest - middle.astype(jnp.float32)).astype(jnp.bfloat16)
    return high, middle, low


def observed_kernel(values_ref, precision_ref, index_ref, out_ref):
    count = index_ref.shape[1]
    width = out_ref.shape[1]
    parts = list(split(precision_ref[...])) + list(split(values_ref[...]))
    pad = jnp.zeros((16 - len(parts), count), jnp.bfloat16)
    rows = jnp.concatenate(parts + [pad], axis=0)
    position = lax.broadcasted_iota(jnp.int32, (width, count), 0)
    hit = (position == index_ref[...]).astype(jnp.float32).astype(jnp.bfloat16)
    placed = lax.dot_general(
        rows, hit, (((1,), (1,)), ((), ())), preferred_element_type=jnp.float32
    )
    out_ref[0:1, :] = placed[0:1] + placed[1:2] + placed[2:3]
    out_ref[1:2, :] = placed[3:4] + placed[4:5] + placed[5:6]
    out_ref[2:8, :] = jnp.zeros((6, width), jnp.float32)


def gram_kernel(dims, forecast_ref, observed_ref, out_ref, scaled_ref):
    clusters, terms, members, cols = dims
    total = clusters * members
    scale = 1.0 / math.sqrt(total - 1)
    half = LANES
    for term in range(terms):
        at = slice(term * cols, (term + 1) * cols)
        values = forecast_ref[:, term].reshape(total, cols)
        mean = jnp.sum(values, axis=0, keepdims=True) * (1.0 / total)
        weight = observed_ref[0:1, at] * scale
        scaled_ref[0:total, at] = (values - mean) * weight
        innovation = (observed_ref[1:2, at] - mean) * weight
        scaled_ref[total : total + 8, at] = jnp.concatenate(
            [innovation, jnp.zeros((7, cols), jnp.float32)], axis=0
        )
    product = lax.dot_general(
        scaled_ref[...],
        scaled_ref[0:total, :],
        (((1,), (1,)), ((), ())),
        precision=lax.Precision.HIGHEST,
        preferred_element_type=jnp.float32,
    )
    at = 0
    for first in range(0, total, half):
        out_ref[at : at + total - first, :] = product[first:total, first : first + half]
        at += total - first
    for k, first in enumerate(range(0, total, half)):
        out_ref[at + 8 * k : at + 8 * k + 8, :] = product[total : total + 8, first : first + half]
    at += 8 * (total // half)
    if at < out_ref.shape[0]:
        out_ref[at:, :] = jnp.zeros((out_ref.shape[0] - at, half), jnp.float32)


def flip(value, axis, bits):
    return lax.ppermute(value, axis, [(i, i ^ bits) for i in range(lax.axis_size(axis))])


def total_over_devices(value):
    sizes = tuple(lax.axis_size(axis) for axis in ("group", "member", "space"))
    if sizes != (4, 2, 4):
        return lax.psum(value, ("group", "member", "space"))
    rows, cols = value.shape
    core = lax.axis_index("member")
    chip = lax.axis_index("group")
    half = rows // 2
    part = half // 4
    kept = lax.dynamic_slice_in_dim(value, core * half, half, 0)
    given = lax.dynamic_slice_in_dim(value, (1 - core) * half, half, 0)
    summed = (kept + flip(given, "member", 1)).reshape(4, part, cols)
    pieces = [lax.dynamic_index_in_dim(summed, chip ^ s, 0, False) for s in range(4)]
    piece = pieces[0] + (
        flip(pieces[1], "group", 1) + flip(pieces[2], "group", 2) + flip(pieces[3], "group", 3)
    )
    piece = piece + (flip(piece, "space", 1) + flip(piece, "space", 2) + flip(piece, "space", 3))
    got = jnp.stack([piece] + [flip(piece, "group", s) for s in (1, 2, 3)], axis=0)
    mine = jnp.concatenate(
        [lax.dynamic_index_in_dim(got, chip ^ i, 0, False) for i in range(4)], axis=0
    )
    other = flip(mine, "member", 1)
    return jnp.concatenate(
        [jnp.where(core == 0, mine, other), jnp.where(core == 0, other, mine)], axis=0
    )


def product(left, right, contract):
    return lax.dot_general(
        left,
        right,
        (contract, ((), ())),
        precision=lax.Precision.HIGHEST,
        preferred_element_type=jnp.float32,
    )


def inverse_factor(block):
    size = block.shape[0]
    tile = 8
    count = size // tile
    rows = [block[at : at + tile, :] for at in range(0, size, tile)]
    lane = lax.broadcasted_iota(jnp.int32, (tile, size), 1)
    sublane = lax.broadcasted_iota(jnp.int32, (tile, size), 0)

    def row(value, at):
        return jnp.broadcast_to(value[at : at + 1, :], (tile, size))

    def column(value, at):
        return jnp.broadcast_to(value[:, at : at + 1], (tile, size))

    for own in range(count):
        start = own * tile
        columns = [[column(value, start + k) for k in range(tile)] for value in rows[own:]]
        pivots = (lane >= start) & (lane < start + tile)
        cleared = [jnp.where(pivots, 0.0, value) for value in rows[own:]]
        local = columns[0]
        right = jnp.where(lane - start == sublane, 1.0, cleared[0])
        done = right
        solved = []
        for p in range(0, tile, 2):
            s00, s10, s11 = row(local[p], p), row(local[p], p + 1), row(local[p + 1], p + 1)
            inv0 = 1.0 / s00
            inv1 = s00 * (1.0 / (s00 * s11 - s10 * s10))
            low = s10 * inv0
            upper = []
            for k in range(p + 2, tile):
                u0 = row(local[k], p)
                upper.append((u0 * inv0, (row(local[k], p + 1) - low * u0) * inv1))
            r0 = row(right, p)
            r1 = row(right, p + 1) - low * r0
            solved += [r0 * inv0, r1 * inv1]
            done = jnp.where(sublane == p, r0 * lax.rsqrt(s00), done)
            done = jnp.where(sublane == p + 1, r1 * (inv1 * lax.rsqrt(inv1)), done)
            for value in columns:
                value[p + 1] = value[p + 1] - low * value[p]
                for k, (u0, u1) in zip(range(p + 2, tile), upper):
                    value[k] = value[k] - (value[p] * u0 + value[p + 1] * u1)
            if p + 2 < tile:
                right = right - (local[p] * solved[p] + local[p + 1] * solved[p + 1])
        rows[own] = jnp.where(lane - start <= sublane, done, 0.0)
        for k in range(own + 1, count):
            terms = [left * value for left, value in zip(columns[k - own], solved)]
            while len(terms) > 1:
                terms = [x + y for x, y in zip(terms[::2], terms[1::2])]
            rows[k] = cleared[k - own] - terms[0]
    return jnp.concatenate(rows, axis=0)


def transform_of(packed_ref, total):
    half = LANES
    count = total // half
    ROWS, LAST = ((1,), (0,)), ((1,), (1,))
    gram, at = {}, 0
    for column in range(count):
        for row in range(column, count):
            gram[row, column] = packed_ref[at : at + half, :]
            at += half
    pull = [packed_ref[at + 8 * k : at + 8 * k + 1, :] for k in range(count)]
    diagonal = lax.broadcasted_iota(jnp.int32, (half, half), 0) == lax.broadcasted_iota(
        jnp.int32, (half, half), 1
    )
    identity = jnp.where(diagonal, 1.0, 0.0)
    factor, inverse = {}, {}
    for column in range(count):
        for row in range(column, count):
            left = gram[row, column]
            if row == column:
                left = left + identity
            for k in range(column):
                left = left - product(factor[row, k], factor[column, k], LAST)
            if row == column:
                inverse[row, row] = inverse_factor(left)
            else:
                factor[row, column] = product(left, inverse[column, column], LAST)
    for row in range(count):
        for column in range(row):
            total_term = product(factor[row, column], inverse[column, column], ROWS)
            for k in range(column + 1, row):
                total_term = total_term + product(factor[row, k], inverse[k, column], ROWS)
            inverse[row, column] = -product(inverse[row, row], total_term, ROWS)
    inner = [
        sum(
            jnp.sum(inverse[row, column] * pull[column], axis=1, keepdims=True)
            for column in range(row + 1)
        )
        for row in range(count)
    ]
    weights = [
        sum(
            jnp.sum(inverse[row, column] * inner[row], axis=0, keepdims=True)
            for row in range(column, count)
        )
        for column in range(count)
    ]
    zero = jnp.zeros((half, half), jnp.float32)
    return jnp.concatenate(
        [
            jnp.concatenate(
                [inverse.get((row, column), zero) + weights[column] for column in range(count)],
                axis=1,
            )
            for row in range(count)
        ],
        axis=0,
    )


def update_kernel(dims, forecast_ref, packed_ref, out_ref, transform_ref):
    clusters, terms, members, cols = dims
    total = clusters * members
    transform_ref[...] = transform_of(packed_ref, total)
    transform = transform_ref[...]
    step = 2
    for first in range(0, terms, step):
        some = range(first, min(first + step, terms))
        values = [forecast_ref[:, term].reshape(total, cols) for term in some]
        means = [jnp.sum(v, axis=0, keepdims=True) * (1.0 / total) for v in values]
        anomaly = jnp.concatenate([v - m for v, m in zip(values, means)], axis=1)
        updated = product(transform, anomaly, ((1,), (0,))) + jnp.concatenate(means, axis=1)
        for k, term in enumerate(some):
            out_ref[:, term] = updated[:, k * cols : (k + 1) * cols].reshape(clusters, members, cols)


def place_kernel(dims, in_ref, out_ref):
    clusters, fields, block_rows, members, cols = dims
    rows = clusters * block_rows
    for cluster in range(clusters):
        for field in range(fields):
            for row in range(block_rows):
                at = field * rows + cluster * block_rows + row
                out_ref[pl.ds(at, members, stride=fields * rows), :] = in_ref[
                    cluster, field * block_rows + row
                ]


def on_device(state, obs_values, obs_precision, obs_index):
    members, fields, rows, cols = state.shape
    clusters = lax.axis_size("group") * lax.axis_size("member")
    block_rows = rows // clusters
    terms = fields * block_rows
    total = clusters * members
    dims = (clusters, terms, members, cols)
    predicted = forecast(state, clusters)
    arrived = lax.all_to_all(predicted, ("group", "member"), split_axis=0, concat_axis=0, tiled=True)
    observed = call(observed_kernel, f32(8, terms * cols), 3)(obs_values, obs_precision, obs_index)
    packed = call(
        functools.partial(gram_kernel, dims),
        f32(448, LANES),
        2,
        [pltpu.VMEM((total + 8, terms * cols), jnp.float32)],
    )(arrived, observed)
    packed = total_over_devices(packed)
    updated = call(
        functools.partial(update_kernel, dims),
        f32(clusters, terms, members, cols),
        2,
        [pltpu.VMEM((total, total), jnp.float32)],
    )(arrived, packed)
    returned = lax.all_to_all(updated, ("group", "member"), split_axis=0, concat_axis=0, tiled=True)
    placed = call(
        functools.partial(place_kernel, (clusters, fields, block_rows, members, cols)),
        f32(members * fields * rows, cols),
        1,
    )(returned)
    return placed.reshape(members, fields, rows, cols)


def solution(mesh):
    blocks = P(("group", "member", "space"), None)
    state = P(("group", "member"), None, "space", None)
    return jax.shard_map(
        on_device,
        mesh=mesh,
        in_specs=(state, blocks, blocks, blocks),
        out_specs=state,
        check_vma=False,
    )
```

```python
import functools
import math

import jax
import jax.numpy as jnp
from jax import lax
from jax.experimental import pallas as pl
from jax.experimental.pallas import tpu as pltpu
from jax.sharding import PartitionSpec as P

STEPS = 2
GRAV = 0.4
DEPTH = 0.4
HALO = (4, 3, 2)
HALO_ROWS = sum(HALO)
LANES = 128
DIRECT = 8
VMEM_LIMIT = 40 * 1024 * 1024


def whole(shape, memory_space=pltpu.VMEM):
    return pl.BlockSpec(memory_space=memory_space)


def call(kernel, out_shape, n_in, scratch=(), **kw):
    single = not isinstance(out_shape, (list, tuple))
    n_out = 1 if single else len(out_shape)
    spec = pl.BlockSpec(memory_space=pltpu.VMEM)
    return pl.pallas_call(
        kernel,
        out_shape=out_shape,
        in_specs=[spec] * n_in,
        out_specs=spec if single else [spec] * n_out,
        scratch_shapes=list(scratch),
        compiler_params=pltpu.CompilerParams(vmem_limit_bytes=VMEM_LIMIT),
        **kw,
    )


def f32(*shape):
    return jax.ShapeDtypeStruct(shape, jnp.float32)


def pack_kernel(top_ref, bottom_ref, to_prev_ref, to_next_ref):
    fields, edge = top_ref.shape[1], top_ref.shape[2]
    at = 0
    for field, rows in enumerate(HALO):
        for row in range(rows):
            to_prev_ref[at] = top_ref[:, field, row, :]
            to_next_ref[at] = bottom_ref[:, field, edge - rows + row, :]
            at += 1


def pack_edges(state):
    members, fields, rows, cols = state.shape
    edge = 8
    last = rows // edge - 1
    block = (members, fields, edge, cols)
    out = f32(HALO_ROWS, members, cols)
    out_spec = pl.BlockSpec((HALO_ROWS, members, cols), lambda i: (0, 0, 0))
    return pl.pallas_call(
        pack_kernel,
        grid=(1,),
        out_shape=[out, out],
        in_specs=[
            pl.BlockSpec(block, lambda i: (0, 0, 0, 0)),
            pl.BlockSpec(block, lambda i: (0, 0, last, 0)),
        ],
        out_specs=[out_spec, out_spec],
        compiler_params=pltpu.CompilerParams(vmem_limit_bytes=VMEM_LIMIT),
    )(state, state)


def sweep(first, last, rows, cols, load, store, inside):
    def across_y(value):
        return pltpu.roll(value, cols - 1, 1) - pltpu.roll(value, 1, 1)

    height, height_1 = {}, {}
    flow_x1, flow_y1, flow_x2, flow_y2 = {}, {}, {}, {}
    height[first - 4] = load(0, first - 4)
    height[first - 3] = load(0, first - 3)
    for lead in range(first - 3, last + 7):
        row = lead
        if row < last + 3:
            height[row + 1] = load(0, row + 1)
            flow_x1[row] = inside(
                load(1, row) - GRAV * (height[row + 1] - height[row - 1]), row
            )
            if first - 2 <= row < last + 2:
                flow_y1[row] = load(2, row) - GRAV * across_y(height[row])
        row = lead - 1
        if first - 2 <= row < last + 2:
            height_1[row] = inside(
                height[row]
                - DEPTH * (flow_x1[row + 1] - flow_x1[row - 1] + across_y(flow_y1[row])),
                row,
            )
        row = lead - 2
        if first - 1 <= row < last + 1:
            flow_x2[row] = inside(
                flow_x1[row] - GRAV * (height_1[row + 1] - height_1[row - 1]), row
            )
            if first <= row < last:
                flow_y2[row] = flow_y1[row] - GRAV * across_y(height_1[row])
                store(1, row, flow_x2[row])
                store(2, row, flow_y2[row])
        row = lead - 3
        if first <= row < last:
            store(
                0,
                row,
                height_1[row]
                - DEPTH * (flow_x2[row + 1] - flow_x2[row - 1] + across_y(flow_y2[row])),
            )


def interior_kernel(dims, state_ref, out_ref):
    members, fields, rows, cols, block_rows, edge = dims
    for at in range(0, members, 8):

        def load(field, row):
            start = (at * fields + field) * rows + row
            return state_ref[pl.ds(start, 8, stride=fields * rows), :]

        def store(field, row, value):
            block, within = divmod(row, block_rows)
            out_ref[block, field * block_rows + within, at : at + 8, :] = value

        sweep(edge, rows - edge, rows, cols, load, store, lambda value, row: value)


def own_cluster(clusters):
    if clusters > DIRECT:
        return 0
    return lax.axis_index("group") * lax.axis_size("member") + lax.axis_index("member")


def edge_kernel(dims, state_ref, before_ref, after_ref, interior_ref, *refs):
    members, fields, rows, cols, block_rows, edge = dims
    clusters = rows // block_rows
    slots, edges_ref = refs[:clusters], refs[clusters]
    here = lax.axis_index("space")
    has_before = (here > 0).astype(jnp.float32)
    has_after = (here < lax.axis_size("space") - 1).astype(jnp.float32)
    own = own_cluster(clusters)

    def inside(value, row):
        if row < 0:
            return value * has_before
        if row >= rows:
            return value * has_after
        return value

    for at in range(0, members, 8):

        def load(field, row):
            offset = sum(HALO[:field])
            if row < 0:
                return before_ref[offset + HALO[field] + row, at : at + 8, :]
            if row >= rows:
                return after_ref[offset + row - rows, at : at + 8, :]
            start = (at * fields + field) * rows + row
            return state_ref[pl.ds(start, 8, stride=fields * rows), :]

        def store(field, row, value):
            block, within = divmod(row, block_rows)
            edges_ref[block, field * block_rows + within, at : at + 8, :] = value

        sweep(0, edge, rows, cols, load, store, inside)
        sweep(rows - edge, rows, rows, cols, load, store, inside)
    edges_ref[edge // block_rows : clusters - edge // block_rows] = interior_ref[
        edge // block_rows : clusters - edge // block_rows
    ]
    for slot, ref in zip(slot_order(clusters), slots):
        ref[...] = edges_ref[own ^ slot]


def forecast(state, clusters):
    members, fields, rows, cols = state.shape
    block_rows = rows // clusters
    terms = fields * block_rows
    edge = -(-4 // block_rows) * block_rows
    to_prev, to_next = pack_edges(state)
    count = lax.axis_size("space")
    before = lax.ppermute(to_next, "space", [(i, i + 1) for i in range(count - 1)])
    after = lax.ppermute(to_prev, "space", [(i + 1, i) for i in range(count - 1)])
    dims = (members, fields, rows, cols, block_rows, edge)
    flat = state.reshape(members * fields * rows, cols)
    size = members * fields * rows * cols
    interior = call(
        functools.partial(interior_kernel, dims),
        f32(clusters, terms, members, cols),
        1,
        cost_estimate=pl.CostEstimate(
            flops=200 * size, bytes_accessed=16 * size, transcendentals=0
        ),
    )(flat)
    return call(
        functools.partial(edge_kernel, dims),
        [f32(terms, members, cols)] * clusters,
        4,
        [pltpu.VMEM((clusters, terms, members, cols), jnp.float32)],
    )(flat, before, after, interior)


def slot_order(clusters):
    if clusters > DIRECT:
        return list(range(clusters))
    cores = lax.axis_size("member")
    return [0] + sorted(range(1, clusters), key=lambda s: (s < cores, s % cores, s))


def exchange(slots):
    clusters = len(slots)
    if clusters > DIRECT:
        stacked = jnp.stack(slots, axis=0)
        got = lax.all_to_all(stacked, ("group", "member"), split_axis=0, concat_axis=0, tiled=True)
        return [got[k] for k in range(clusters)]
    got = [slots[0]]
    for slot, value in list(zip(slot_order(clusters), slots))[1:]:
        pairs = [(i, i ^ slot) for i in range(clusters)]
        got.append(lax.ppermute(value, ("group", "member"), pairs))
    return got


def split(value):
    high = value.astype(jnp.bfloat16)
    rest = value - high.astype(jnp.float32)
    middle = rest.astype(jnp.bfloat16)
    low = (rest - middle.astype(jnp.float32)).astype(jnp.bfloat16)
    return high, middle, low


def observed_kernel(values_ref, precision_ref, index_ref, out_ref):
    count = index_ref.shape[1]
    width = out_ref.shape[1]
    parts = list(split(precision_ref[...])) + list(split(values_ref[...]))
    pad = jnp.zeros((16 - len(parts), count), jnp.bfloat16)
    rows = jnp.concatenate(parts + [pad], axis=0)
    position = lax.broadcasted_iota(jnp.int32, (width, count), 0)
    hit = (position == index_ref[...]).astype(jnp.float32).astype(jnp.bfloat16)
    placed = lax.dot_general(
        rows, hit, (((1,), (1,)), ((), ())), preferred_element_type=jnp.float32
    )
    out_ref[0:1, :] = placed[0:1] + placed[1:2] + placed[2:3]
    out_ref[1:2, :] = placed[3:4] + placed[4:5] + placed[5:6]
    out_ref[2:8, :] = jnp.zeros((6, width), jnp.float32)


def gram_kernel(dims, observed_ref, *refs):
    clusters, terms, members, cols = dims
    arrived, (out_ref, anomaly_ref, mean_ref, scaled_ref) = refs[:clusters], refs[clusters:]
    total = clusters * members
    scale = 1.0 / math.sqrt(total - 1)
    half = LANES
    own = own_cluster(clusters)
    places = [pl.multiple_of((own ^ slot) * members, members) for slot in slot_order(clusters)]
    for term in range(terms):
        at = slice(term * cols, (term + 1) * cols)
        values = [ref[term] for ref in arrived]
        summed = values[0]
        for value in values[1:]:
            summed = summed + value
        mean = jnp.sum(summed, axis=0, keepdims=True) * (1.0 / total)
        mean_ref[:, at] = jnp.broadcast_to(mean, (8, cols))
        weight = observed_ref[0:1, at] * scale
        for place, value in zip(places, values):
            anomaly = value - mean
            anomaly_ref[pl.ds(place, members), at] = anomaly
            scaled_ref[pl.ds(place, members), at] = anomaly * weight
        innovation = (observed_ref[1:2, at] - mean) * weight
        scaled_ref[total : total + 8, at] = jnp.concatenate(
            [innovation, jnp.zeros((7, cols), jnp.float32)], axis=0
        )
    result = product(scaled_ref[...], scaled_ref[0:total, :], ((1,), (1,)))
    at = 0
    for first in range(0, total, half):
        out_ref[at : at + total - first, :] = result[first:total, first : first + half]
        at += total - first
    for k, first in enumerate(range(0, total, half)):
        out_ref[at + 8 * k : at + 8 * k + 8, :] = result[total : total + 8, first : first + half]
    at += 8 * (total // half)
    if at < out_ref.shape[0]:
        out_ref[at:, :] = jnp.zeros((out_ref.shape[0] - at, half), jnp.float32)


def flip(value, axis, bits):
    return lax.ppermute(value, axis, [(i, i ^ bits) for i in range(lax.axis_size(axis))])


def total_over_devices(value):
    sizes = tuple(lax.axis_size(axis) for axis in ("group", "member", "space"))
    if sizes != (4, 2, 4):
        return lax.psum(value, ("group", "member", "space"))
    rows, cols = value.shape
    core = lax.axis_index("member")
    chip = lax.axis_index("group")
    half = rows // 2
    part = half // 4
    kept = lax.dynamic_slice_in_dim(value, core * half, half, 0)
    given = lax.dynamic_slice_in_dim(value, (1 - core) * half, half, 0)
    summed = (kept + flip(given, "member", 1)).reshape(4, part, cols)
    pieces = [lax.dynamic_index_in_dim(summed, chip ^ s, 0, False) for s in range(4)]
    piece = pieces[0] + (
        flip(pieces[1], "group", 1) + flip(pieces[2], "group", 2) + flip(pieces[3], "group", 3)
    )
    piece = piece + (flip(piece, "space", 1) + flip(piece, "space", 2) + flip(piece, "space", 3))
    got = jnp.stack([piece] + [flip(piece, "group", s) for s in (1, 2, 3)], axis=0)
    mine = jnp.concatenate(
        [lax.dynamic_index_in_dim(got, chip ^ i, 0, False) for i in range(4)], axis=0
    )
    other = flip(mine, "member", 1)
    return jnp.concatenate(
        [jnp.where(core == 0, mine, other), jnp.where(core == 0, other, mine)], axis=0
    )


def product(left, right, contract):
    return lax.dot_general(
        left,
        right,
        (contract, ((), ())),
        precision=lax.Precision.HIGHEST,
        preferred_element_type=jnp.float32,
    )


def inverse_factor(block):
    size = block.shape[0]
    tile = 8
    count = size // tile
    rows = [block[at : at + tile, :] for at in range(0, size, tile)]
    lane = lax.broadcasted_iota(jnp.int32, (tile, size), 1)
    sublane = lax.broadcasted_iota(jnp.int32, (tile, size), 0)

    def row(value, at):
        return jnp.broadcast_to(value[at : at + 1, :], (tile, size))

    def column(value, at):
        return jnp.broadcast_to(value[:, at : at + 1], (tile, size))

    for own in range(count):
        start = own * tile
        columns = [[column(value, start + k) for k in range(tile)] for value in rows[own:]]
        pivots = (lane >= start) & (lane < start + tile)
        cleared = [jnp.where(pivots, 0.0, value) for value in rows[own:]]
        local = columns[0]
        right = jnp.where(lane - start == sublane, 1.0, cleared[0])
        done = right
        solved = []
        for p in range(0, tile, 2):
            s00, s10, s11 = row(local[p], p), row(local[p], p + 1), row(local[p + 1], p + 1)
            inv0 = 1.0 / s00
            inv1 = s00 * (1.0 / (s00 * s11 - s10 * s10))
            low = s10 * inv0
            upper = []
            for k in range(p + 2, tile):
                u0 = row(local[k], p)
                upper.append((u0 * inv0, (row(local[k], p + 1) - low * u0) * inv1))
            r0 = row(right, p)
            r1 = row(right, p + 1) - low * r0
            solved += [r0 * inv0, r1 * inv1]
            done = jnp.where(sublane == p, r0 * lax.rsqrt(s00), done)
            done = jnp.where(sublane == p + 1, r1 * (inv1 * lax.rsqrt(inv1)), done)
            for value in columns:
                value[p + 1] = value[p + 1] - low * value[p]
                for k, (u0, u1) in zip(range(p + 2, tile), upper):
                    value[k] = value[k] - (value[p] * u0 + value[p + 1] * u1)
            if p + 2 < tile:
                right = right - (local[p] * solved[p] + local[p + 1] * solved[p + 1])
        rows[own] = jnp.where(lane - start <= sublane, done, 0.0)
        for k in range(own + 1, count):
            terms = [left * value for left, value in zip(columns[k - own], solved)]
            while len(terms) > 1:
                terms = [x + y for x, y in zip(terms[::2], terms[1::2])]
            rows[k] = cleared[k - own] - terms[0]
    return jnp.concatenate(rows, axis=0)


def transform_of(packed_ref, total):
    half = LANES
    count = total // half
    ROWS, LAST = ((1,), (0,)), ((1,), (1,))
    gram, at = {}, 0
    for column in range(count):
        for row in range(column, count):
            gram[row, column] = packed_ref[at : at + half, :]
            at += half
    pull = [packed_ref[at + 8 * k : at + 8 * k + 1, :] for k in range(count)]
    diagonal = lax.broadcasted_iota(jnp.int32, (half, half), 0) == lax.broadcasted_iota(
        jnp.int32, (half, half), 1
    )
    identity = jnp.where(diagonal, 1.0, 0.0)
    factor, inverse = {}, {}
    for column in range(count):
        for row in range(column, count):
            left = gram[row, column]
            if row == column:
                left = left + identity
            for k in range(column):
                left = left - product(factor[row, k], factor[column, k], LAST)
            if row == column:
                inverse[row, row] = inverse_factor(left)
            else:
                factor[row, column] = product(left, inverse[column, column], LAST)
    for row in range(count):
        for column in range(row):
            total_term = product(factor[row, column], inverse[column, column], ROWS)
            for k in range(column + 1, row):
                total_term = total_term + product(factor[row, k], inverse[k, column], ROWS)
            inverse[row, column] = -product(inverse[row, row], total_term, ROWS)
    inner = [
        sum(
            jnp.sum(inverse[row, column] * pull[column], axis=1, keepdims=True)
            for column in range(row + 1)
        )
        for row in range(count)
    ]
    weights = [
        sum(
            jnp.sum(inverse[row, column] * inner[row], axis=0, keepdims=True)
            for row in range(column, count)
        )
        for column in range(count)
    ]
    zero = jnp.zeros((half, half), jnp.float32)
    return jnp.concatenate(
        [
            jnp.concatenate(
                [inverse.get((row, column), zero) + weights[column] for column in range(count)],
                axis=1,
            )
            for row in range(count)
        ],
        axis=0,
    )


def update_kernel(dims, anomaly_ref, mean_ref, packed_ref, *refs):
    clusters, terms, members, cols = dims
    slots, transform_ref = refs[:clusters], refs[clusters]
    total = clusters * members
    own = own_cluster(clusters)
    transform_ref[...] = transform_of(packed_ref, total)
    transform = jnp.concatenate(
        [
            transform_ref[pl.ds(pl.multiple_of((own ^ slot) * members, members), members), :]
            for slot in slot_order(clusters)
        ],
        axis=0,
    )
    step = 2 * cols
    width = terms * cols
    for first in range(0, width, step):
        at = slice(first, min(first + step, width))
        updated = product(transform, anomaly_ref[:, at], ((1,), (0,))) + mean_ref[0:1, at]
        for k in range((at.stop - first) // cols):
            for at_slot, ref in enumerate(slots):
                ref[first // cols + k] = updated[
                    at_slot * members : (at_slot + 1) * members, k * cols : (k + 1) * cols
                ]


def place_kernel(dims, *refs):
    clusters, fields, block_rows, cols = dims
    slots, out_ref = refs[:clusters], refs[clusters]
    rows = clusters * block_rows
    own = own_cluster(clusters)
    for slot, ref in zip(slot_order(clusters), slots):
        first = (own ^ slot) * block_rows
        for field in range(fields):
            for row in range(block_rows):
                at = field * rows + row + first
                out_ref[pl.ds(at, 8, stride=fields * rows), :] = ref[field * block_rows + row]


def place(slots, fields):
    clusters = len(slots)
    terms, members, cols = slots[0].shape
    rows = clusters * terms
    return pl.pallas_call(
        functools.partial(place_kernel, (clusters, fields, terms // fields, cols)),
        grid=(members // 8,),
        out_shape=f32(members * rows, cols),
        in_specs=[pl.BlockSpec((terms, 8, cols), lambda i: (0, i, 0))] * clusters,
        out_specs=pl.BlockSpec((8 * rows, cols), lambda i: (i, 0)),
        compiler_params=pltpu.CompilerParams(vmem_limit_bytes=VMEM_LIMIT),
    )(*slots)


def on_device(state, obs_values, obs_precision, obs_index):
    members, fields, rows, cols = state.shape
    clusters = lax.axis_size("group") * lax.axis_size("member")
    terms = fields * (rows // clusters)
    total = clusters * members
    width = terms * cols
    dims = (clusters, terms, members, cols)
    arrived = exchange(forecast(state, clusters))
    observed = call(observed_kernel, f32(8, width), 3)(obs_values, obs_precision, obs_index)
    packed, anomaly, mean = call(
        functools.partial(gram_kernel, dims),
        [f32(448, LANES), f32(total, width), f32(8, width)],
        1 + clusters,
        [pltpu.VMEM((total + 8, width), jnp.float32)],
    )(observed, *arrived)
    packed = total_over_devices(packed)
    updated = call(
        functools.partial(update_kernel, dims),
        [f32(terms, members, cols)] * clusters,
        3,
        [pltpu.VMEM((total, total), jnp.float32)],
    )(anomaly, mean, packed)
    return place(exchange(updated), fields).reshape(members, fields, rows, cols)


def solution(mesh):
    blocks = P(("group", "member", "space"), None)
    state = P(("group", "member"), None, "space", None)
    return jax.shard_map(
        on_device,
        mesh=mesh,
        in_specs=(state, blocks, blocks, blocks),
        out_specs=state,
        check_vma=False,
    )
```

```python
import functools
import math

import jax
import jax.numpy as jnp
from jax import lax
from jax.experimental import pallas as pl
from jax.experimental.pallas import tpu as pltpu
from jax.sharding import PartitionSpec as P

STEPS = 2
GRAV = 0.4
DEPTH = 0.4
HALO = (4, 3, 2)
HALO_ROWS = sum(HALO)
LANES = 128
DIRECT = 8
VMEM_LIMIT = 40 * 1024 * 1024


def whole(shape, memory_space=pltpu.VMEM):
    return pl.BlockSpec(memory_space=memory_space)


def call(kernel, out_shape, n_in, scratch=(), **kw):
    single = not isinstance(out_shape, (list, tuple))
    n_out = 1 if single else len(out_shape)
    spec = pl.BlockSpec(memory_space=pltpu.VMEM)
    return pl.pallas_call(
        kernel,
        out_shape=out_shape,
        in_specs=[spec] * n_in,
        out_specs=spec if single else [spec] * n_out,
        scratch_shapes=list(scratch),
        compiler_params=pltpu.CompilerParams(vmem_limit_bytes=VMEM_LIMIT),
        **kw,
    )


def f32(*shape):
    return jax.ShapeDtypeStruct(shape, jnp.float32)


def pack_kernel(top_ref, bottom_ref, to_prev_ref, to_next_ref):
    fields, edge = top_ref.shape[1], top_ref.shape[2]
    at = 0
    for field, rows in enumerate(HALO):
        for row in range(rows):
            to_prev_ref[at] = top_ref[:, field, row, :]
            to_next_ref[at] = bottom_ref[:, field, edge - rows + row, :]
            at += 1


def pack_edges(state):
    members, fields, rows, cols = state.shape
    edge = 8
    last = rows // edge - 1
    block = (members, fields, edge, cols)
    out = f32(HALO_ROWS, members, cols)
    out_spec = pl.BlockSpec((HALO_ROWS, members, cols), lambda i: (0, 0, 0))
    return pl.pallas_call(
        pack_kernel,
        grid=(1,),
        out_shape=[out, out],
        in_specs=[
            pl.BlockSpec(block, lambda i: (0, 0, 0, 0)),
            pl.BlockSpec(block, lambda i: (0, 0, last, 0)),
        ],
        out_specs=[out_spec, out_spec],
        compiler_params=pltpu.CompilerParams(vmem_limit_bytes=VMEM_LIMIT),
    )(state, state)


def sweep(first, last, rows, cols, load, store, inside):
    def across_y(value):
        return pltpu.roll(value, cols - 1, 1) - pltpu.roll(value, 1, 1)

    height, height_1 = {}, {}
    flow_x1, flow_y1, flow_x2, flow_y2 = {}, {}, {}, {}
    height[first - 4] = load(0, first - 4)
    height[first - 3] = load(0, first - 3)
    for lead in range(first - 3, last + 7):
        row = lead
        if row < last + 3:
            height[row + 1] = load(0, row + 1)
            flow_x1[row] = inside(
                load(1, row) - GRAV * (height[row + 1] - height[row - 1]), row
            )
            if first - 2 <= row < last + 2:
                flow_y1[row] = load(2, row) - GRAV * across_y(height[row])
        row = lead - 1
        if first - 2 <= row < last + 2:
            height_1[row] = inside(
                height[row]
                - DEPTH * (flow_x1[row + 1] - flow_x1[row - 1] + across_y(flow_y1[row])),
                row,
            )
        row = lead - 2
        if first - 1 <= row < last + 1:
            flow_x2[row] = inside(
                flow_x1[row] - GRAV * (height_1[row + 1] - height_1[row - 1]), row
            )
            if first <= row < last:
                flow_y2[row] = flow_y1[row] - GRAV * across_y(height_1[row])
                store(1, row, flow_x2[row])
                store(2, row, flow_y2[row])
        row = lead - 3
        if first <= row < last:
            store(
                0,
                row,
                height_1[row]
                - DEPTH * (flow_x2[row + 1] - flow_x2[row - 1] + across_y(flow_y2[row])),
            )


def interior_kernel(dims, state_ref, out_ref):
    members, fields, rows, cols, block_rows, edge = dims
    for at in range(0, members, 8):

        def load(field, row):
            start = (at * fields + field) * rows + row
            return state_ref[pl.ds(start, 8, stride=fields * rows), :]

        def store(field, row, value):
            block, within = divmod(row, block_rows)
            out_ref[block, field * block_rows + within, at : at + 8, :] = value

        sweep(edge, rows - edge, rows, cols, load, store, lambda value, row: value)


def own_cluster(clusters):
    if clusters > DIRECT:
        return 0
    return lax.axis_index("group") * lax.axis_size("member") + lax.axis_index("member")


def edge_kernel(dims, state_ref, before_ref, after_ref, interior_ref, *refs):
    members, fields, rows, cols, block_rows, edge = dims
    clusters = rows // block_rows
    slots, edges_ref = refs[:clusters], refs[clusters]
    here = lax.axis_index("space")
    has_before = (here > 0).astype(jnp.float32)
    has_after = (here < lax.axis_size("space") - 1).astype(jnp.float32)
    own = own_cluster(clusters)

    def inside(value, row):
        if row < 0:
            return value * has_before
        if row >= rows:
            return value * has_after
        return value

    for at in range(0, members, 8):

        def load(field, row):
            offset = sum(HALO[:field])
            if row < 0:
                return before_ref[offset + HALO[field] + row, at : at + 8, :]
            if row >= rows:
                return after_ref[offset + row - rows, at : at + 8, :]
            start = (at * fields + field) * rows + row
            return state_ref[pl.ds(start, 8, stride=fields * rows), :]

        def store(field, row, value):
            block, within = divmod(row, block_rows)
            edges_ref[block, field * block_rows + within, at : at + 8, :] = value

        sweep(0, edge, rows, cols, load, store, inside)
        sweep(rows - edge, rows, rows, cols, load, store, inside)
    edges_ref[edge // block_rows : clusters - edge // block_rows] = interior_ref[
        edge // block_rows : clusters - edge // block_rows
    ]
    for slot, ref in zip(slot_order(clusters), slots):
        ref[...] = edges_ref[own ^ slot]


def forecast(state, clusters):
    members, fields, rows, cols = state.shape
    block_rows = rows // clusters
    terms = fields * block_rows
    edge = -(-4 // block_rows) * block_rows
    to_prev, to_next = pack_edges(state)
    count = lax.axis_size("space")
    before = lax.ppermute(to_next, "space", [(i, i + 1) for i in range(count - 1)])
    after = lax.ppermute(to_prev, "space", [(i + 1, i) for i in range(count - 1)])
    dims = (members, fields, rows, cols, block_rows, edge)
    flat = state.reshape(members * fields * rows, cols)
    size = members * fields * rows * cols
    interior = call(
        functools.partial(interior_kernel, dims),
        f32(clusters, terms, members, cols),
        1,
        cost_estimate=pl.CostEstimate(
            flops=200 * size, bytes_accessed=16 * size, transcendentals=0
        ),
    )(flat)
    return call(
        functools.partial(edge_kernel, dims),
        [f32(terms, members, cols)] * clusters,
        4,
        [pltpu.VMEM((clusters, terms, members, cols), jnp.float32)],
    )(flat, before, after, interior)


def slot_order(clusters):
    if clusters > DIRECT:
        return list(range(clusters))
    cores = lax.axis_size("member")
    return [0] + sorted(range(1, clusters), key=lambda s: (s < cores, s % cores, s))


def exchange(slots):
    clusters = len(slots)
    if clusters > DIRECT:
        stacked = jnp.stack(slots, axis=0)
        got = lax.all_to_all(stacked, ("group", "member"), split_axis=0, concat_axis=0, tiled=True)
        return [got[k] for k in range(clusters)]
    got = [slots[0]]
    for slot, value in list(zip(slot_order(clusters), slots))[1:]:
        pairs = [(i, i ^ slot) for i in range(clusters)]
        got.append(lax.ppermute(value, ("group", "member"), pairs))
    return got


def split(value):
    high = value.astype(jnp.bfloat16)
    rest = value - high.astype(jnp.float32)
    middle = rest.astype(jnp.bfloat16)
    low = (rest - middle.astype(jnp.float32)).astype(jnp.bfloat16)
    return high, middle, low


def observed_kernel(values_ref, precision_ref, index_ref, out_ref):
    count = index_ref.shape[1]
    width = out_ref.shape[1]
    parts = list(split(precision_ref[...])) + list(split(values_ref[...]))
    pad = jnp.zeros((16 - len(parts), count), jnp.bfloat16)
    rows = jnp.concatenate(parts + [pad], axis=0)
    position = lax.broadcasted_iota(jnp.int32, (width, count), 0)
    hit = (position == index_ref[...]).astype(jnp.float32).astype(jnp.bfloat16)
    placed = lax.dot_general(
        rows, hit, (((1,), (1,)), ((), ())), preferred_element_type=jnp.float32
    )
    out_ref[0:1, :] = placed[0:1] + placed[1:2] + placed[2:3]
    out_ref[1:2, :] = placed[3:4] + placed[4:5] + placed[5:6]
    out_ref[2:8, :] = jnp.zeros((6, width), jnp.float32)


def gram_kernel(dims, observed_ref, *refs):
    clusters, terms, members, cols = dims
    arrived, (out_ref, anomaly_ref, mean_ref, scaled_ref) = refs[:clusters], refs[clusters:]
    total = clusters * members
    scale = 1.0 / math.sqrt(total - 1)
    half = LANES
    own = own_cluster(clusters)
    places = [pl.multiple_of((own ^ slot) * members, members) for slot in slot_order(clusters)]
    for term in range(terms):
        at = slice(term * cols, (term + 1) * cols)
        values = [ref[term] for ref in arrived]
        summed = values[0]
        for value in values[1:]:
            summed = summed + value
        mean = jnp.sum(summed, axis=0, keepdims=True) * (1.0 / total)
        mean_ref[:, at] = jnp.broadcast_to(mean, (8, cols))
        weight = observed_ref[0:1, at] * scale
        for place, value in zip(places, values):
            anomaly = value - mean
            anomaly_ref[pl.ds(place, members), at] = anomaly
            scaled_ref[pl.ds(place, members), at] = anomaly * weight
        innovation = (observed_ref[1:2, at] - mean) * weight
        scaled_ref[total : total + 8, at] = jnp.concatenate(
            [innovation, jnp.zeros((7, cols), jnp.float32)], axis=0
        )
    result = product(scaled_ref[...], scaled_ref[0:total, :], ((1,), (1,)))
    at = 0
    for first in range(0, total, half):
        out_ref[at : at + total - first, :] = result[first:total, first : first + half]
        at += total - first
    for k, first in enumerate(range(0, total, half)):
        out_ref[at + 8 * k : at + 8 * k + 8, :] = result[total : total + 8, first : first + half]
    at += 8 * (total // half)
    if at < out_ref.shape[0]:
        out_ref[at:, :] = jnp.zeros((out_ref.shape[0] - at, half), jnp.float32)


def flip(value, axis, bits):
    return lax.ppermute(value, axis, [(i, i ^ bits) for i in range(lax.axis_size(axis))])


def total_over_devices(value):
    sizes = tuple(lax.axis_size(axis) for axis in ("group", "member", "space"))
    if sizes != (4, 2, 4):
        return lax.psum(value, ("group", "member", "space"))
    rows, cols = value.shape
    core = lax.axis_index("member")
    chip = lax.axis_index("group")
    half = rows // 2
    part = half // 4
    kept = lax.dynamic_slice_in_dim(value, core * half, half, 0)
    given = lax.dynamic_slice_in_dim(value, (1 - core) * half, half, 0)
    summed = (kept + flip(given, "member", 1)).reshape(4, part, cols)
    pieces = [lax.dynamic_index_in_dim(summed, chip ^ s, 0, False) for s in range(4)]
    piece = pieces[0] + (
        flip(pieces[1], "group", 1) + flip(pieces[2], "group", 2) + flip(pieces[3], "group", 3)
    )
    piece = piece + (flip(piece, "space", 3) + flip(piece, "space", 2) + flip(piece, "space", 1))
    got = jnp.stack([piece] + [flip(piece, "group", s) for s in (1, 2, 3)], axis=0)
    mine = jnp.concatenate(
        [lax.dynamic_index_in_dim(got, chip ^ i, 0, False) for i in range(4)], axis=0
    )
    other = flip(mine, "member", 1)
    return jnp.concatenate(
        [jnp.where(core == 0, mine, other), jnp.where(core == 0, other, mine)], axis=0
    )


def product(left, right, contract):
    return lax.dot_general(
        left,
        right,
        (contract, ((), ())),
        precision=lax.Precision.HIGHEST,
        preferred_element_type=jnp.float32,
    )


def eliminate(panel, first):
    tile = 8
    size, width = panel.shape
    count = size // tile
    rows = [panel[at : at + tile, :] for at in range(0, size, tile)]
    lane = lax.broadcasted_iota(jnp.int32, (tile, width), 1)
    sublane = lax.broadcasted_iota(jnp.int32, (tile, width), 0)

    def row(value, at):
        return jnp.broadcast_to(value[at : at + 1, :], (tile, width))

    def column(value, at):
        return jnp.broadcast_to(value[:, at : at + 1], (tile, width))

    ahead = None
    for own in range(count):
        start = first + own * tile
        columns = [[column(value, start + k) for k in range(tile)] for value in rows[own:]]
        if ahead is not None:
            columns[0] = ahead
        if own + 1 < count:
            for value, spread in zip(rows[own : own + 2], columns):
                spread += [column(value, start + k) for k in range(tile, 2 * tile)]
        pivots = (lane >= start) & (lane < start + tile)
        cleared = [jnp.where(pivots, 0.0, value) for value in rows[own:]]
        local = columns[0]
        right = jnp.where(lane - start == sublane, 1.0, cleared[0])
        done = right
        solved = []
        for p in range(0, tile, 2):
            s00, s10, s11 = row(local[p], p), row(local[p], p + 1), row(local[p + 1], p + 1)
            inv0 = 1.0 / s00
            inv1 = s00 * (1.0 / (s00 * s11 - s10 * s10))
            low = s10 * inv0
            upper = []
            for k in range(p + 2, len(local)):
                u0 = row(local[k], p)
                upper.append((u0 * inv0, (row(local[k], p + 1) - low * u0) * inv1))
            r0 = row(right, p)
            r1 = row(right, p + 1) - low * r0
            solved += [r0 * inv0, r1 * inv1]
            done = jnp.where(sublane == p, r0 * lax.rsqrt(s00), done)
            done = jnp.where(sublane == p + 1, r1 * (inv1 * lax.rsqrt(inv1)), done)
            for value in columns:
                value[p + 1] = value[p + 1] - low * value[p]
                for k, (u0, u1) in zip(range(p + 2, len(value)), upper):
                    value[k] = value[k] - (value[p] * u0 + value[p + 1] * u1)
            if p + 2 < tile:
                right = right - (local[p] * solved[p] + local[p + 1] * solved[p + 1])
        rows[own] = jnp.where((lane - start > sublane) & (lane < first + size), 0.0, done)
        if own + 1 < count:
            ahead = columns[1][tile:]
        for k in range(own + 1, count):
            terms = [left * value for left, value in zip(columns[k - own], solved)]
            while len(terms) > 1:
                terms = [x + y for x, y in zip(terms[::2], terms[1::2])]
            rows[k] = cleared[k - own] - terms[0]
    return jnp.concatenate(rows, axis=0)


def inverse_factor(block, panel=64):
    size = block.shape[0]
    done = []
    rest = block
    for first in range(0, size, panel):
        rows = eliminate(rest[:panel], first)
        lane = lax.broadcasted_iota(jnp.int32, rows.shape, 1)
        done.append(jnp.where(lane < first + panel, rows, 0.0))
        if first + panel < size:
            rest = rest[panel:]
            lane = lax.broadcasted_iota(jnp.int32, rest.shape, 1)
            pivots = (lane >= first) & (lane < first + panel)
            change = product(rows, rows, ((0,), (0,)))
            rest = jnp.where(pivots, 0.0, rest) - change[first + panel :]
    return jnp.concatenate(done, axis=0)


def transform_of(packed_ref, total):
    half = LANES
    count = total // half
    ROWS, LAST = ((1,), (0,)), ((1,), (1,))
    gram, at = {}, 0
    for column in range(count):
        for row in range(column, count):
            gram[row, column] = packed_ref[at : at + half, :]
            at += half
    pull = [packed_ref[at + 8 * k : at + 8 * k + 1, :] for k in range(count)]
    diagonal = lax.broadcasted_iota(jnp.int32, (half, half), 0) == lax.broadcasted_iota(
        jnp.int32, (half, half), 1
    )
    identity = jnp.where(diagonal, 1.0, 0.0)
    factor, inverse = {}, {}
    for column in range(count):
        for row in range(column, count):
            left = gram[row, column]
            if row == column:
                left = left + identity
            for k in range(column):
                left = left - product(factor[row, k], factor[column, k], LAST)
            if row == column:
                inverse[row, row] = inverse_factor(left)
            else:
                factor[row, column] = product(left, inverse[column, column], LAST)
    for row in range(count):
        for column in range(row):
            total_term = product(factor[row, column], inverse[column, column], ROWS)
            for k in range(column + 1, row):
                total_term = total_term + product(factor[row, k], inverse[k, column], ROWS)
            inverse[row, column] = -product(inverse[row, row], total_term, ROWS)
    inner = [
        sum(
            jnp.sum(inverse[row, column] * pull[column], axis=1, keepdims=True)
            for column in range(row + 1)
        )
        for row in range(count)
    ]
    weights = [
        sum(
            jnp.sum(inverse[row, column] * inner[row], axis=0, keepdims=True)
            for row in range(column, count)
        )
        for column in range(count)
    ]
    zero = jnp.zeros((half, half), jnp.float32)
    return jnp.concatenate(
        [
            jnp.concatenate(
                [inverse.get((row, column), zero) + weights[column] for column in range(count)],
                axis=1,
            )
            for row in range(count)
        ],
        axis=0,
    )


def update_kernel(dims, anomaly_ref, mean_ref, packed_ref, *refs):
    clusters, terms, members, cols = dims
    slots, transform_ref = refs[:clusters], refs[clusters]
    total = clusters * members
    own = own_cluster(clusters)
    transform_ref[...] = transform_of(packed_ref, total)
    transform = jnp.concatenate(
        [
            transform_ref[pl.ds(pl.multiple_of((own ^ slot) * members, members), members), :]
            for slot in slot_order(clusters)
        ],
        axis=0,
    )
    step = 2 * cols
    width = terms * cols
    for first in range(0, width, step):
        at = slice(first, min(first + step, width))
        updated = product(transform, anomaly_ref[:, at], ((1,), (0,))) + mean_ref[0:1, at]
        for k in range((at.stop - first) // cols):
            for at_slot, ref in enumerate(slots):
                ref[first // cols + k] = updated[
                    at_slot * members : (at_slot + 1) * members, k * cols : (k + 1) * cols
                ]


def place_kernel(dims, *refs):
    clusters, fields, block_rows, cols = dims
    slots, out_ref = refs[:clusters], refs[clusters]
    rows = clusters * block_rows
    own = own_cluster(clusters)
    for slot, ref in zip(slot_order(clusters), slots):
        first = (own ^ slot) * block_rows
        for field in range(fields):
            for row in range(block_rows):
                at = field * rows + row + first
                out_ref[pl.ds(at, 8, stride=fields * rows), :] = ref[field * block_rows + row]


def place(slots, fields):
    clusters = len(slots)
    terms, members, cols = slots[0].shape
    rows = clusters * terms
    return pl.pallas_call(
        functools.partial(place_kernel, (clusters, fields, terms // fields, cols)),
        grid=(members // 8,),
        out_shape=f32(members * rows, cols),
        in_specs=[pl.BlockSpec((terms, 8, cols), lambda i: (0, i, 0))] * clusters,
        out_specs=pl.BlockSpec((8 * rows, cols), lambda i: (i, 0)),
        compiler_params=pltpu.CompilerParams(vmem_limit_bytes=VMEM_LIMIT),
    )(*slots)


def on_device(state, obs_values, obs_precision, obs_index):
    members, fields, rows, cols = state.shape
    clusters = lax.axis_size("group") * lax.axis_size("member")
    terms = fields * (rows // clusters)
    total = clusters * members
    width = terms * cols
    dims = (clusters, terms, members, cols)
    arrived = exchange(forecast(state, clusters))
    observed = call(observed_kernel, f32(8, width), 3)(obs_values, obs_precision, obs_index)
    packed, anomaly, mean = call(
        functools.partial(gram_kernel, dims),
        [f32(448, LANES), f32(total, width), f32(8, width)],
        1 + clusters,
        [pltpu.VMEM((total + 8, width), jnp.float32)],
    )(observed, *arrived)
    packed = total_over_devices(packed)
    updated = call(
        functools.partial(update_kernel, dims),
        [f32(terms, members, cols)] * clusters,
        3,
        [pltpu.VMEM((total, total), jnp.float32)],
    )(anomaly, mean, packed)
    return place(exchange(updated), fields).reshape(members, fields, rows, cols)


def solution(mesh):
    blocks = P(("group", "member", "space"), None)
    state = P(("group", "member"), None, "space", None)
    return jax.shard_map(
        on_device,
        mesh=mesh,
        in_specs=(state, blocks, blocks, blocks),
        out_specs=state,
        check_vma=False,
    )
```

```python
import functools
import math

import jax
import jax.numpy as jnp
from jax import lax
from jax.experimental import pallas as pl
from jax.experimental.pallas import tpu as pltpu
from jax.sharding import PartitionSpec as P

STEPS = 2
GRAV = 0.4
DEPTH = 0.4
HALO = (4, 3, 2)
HALO_ROWS = sum(HALO)
LANES = 128
DIRECT = 8
VMEM_LIMIT = 40 * 1024 * 1024


def whole(shape, memory_space=pltpu.VMEM):
    return pl.BlockSpec(memory_space=memory_space)


def call(kernel, out_shape, n_in, scratch=(), **kw):
    single = not isinstance(out_shape, (list, tuple))
    n_out = 1 if single else len(out_shape)
    spec = pl.BlockSpec(memory_space=pltpu.VMEM)
    return pl.pallas_call(
        kernel,
        out_shape=out_shape,
        in_specs=[spec] * n_in,
        out_specs=spec if single else [spec] * n_out,
        scratch_shapes=list(scratch),
        compiler_params=pltpu.CompilerParams(vmem_limit_bytes=VMEM_LIMIT),
        **kw,
    )


def f32(*shape):
    return jax.ShapeDtypeStruct(shape, jnp.float32)


def pack_kernel(top_ref, bottom_ref, to_prev_ref, to_next_ref):
    fields, edge = top_ref.shape[1], top_ref.shape[2]
    at = 0
    for field, rows in enumerate(HALO):
        for row in range(rows):
            to_prev_ref[at] = top_ref[:, field, row, :]
            to_next_ref[at] = bottom_ref[:, field, edge - rows + row, :]
            at += 1


def pack_edges(state):
    members, fields, rows, cols = state.shape
    edge = 8
    last = rows // edge - 1
    block = (members, fields, edge, cols)
    out = f32(HALO_ROWS, members, cols)
    out_spec = pl.BlockSpec((HALO_ROWS, members, cols), lambda i: (0, 0, 0))
    return pl.pallas_call(
        pack_kernel,
        grid=(1,),
        out_shape=[out, out],
        in_specs=[
            pl.BlockSpec(block, lambda i: (0, 0, 0, 0)),
            pl.BlockSpec(block, lambda i: (0, 0, last, 0)),
        ],
        out_specs=[out_spec, out_spec],
        compiler_params=pltpu.CompilerParams(vmem_limit_bytes=VMEM_LIMIT),
    )(state, state)


def sweep(first, last, rows, cols, load, store, inside):
    def across_y(value):
        return pltpu.roll(value, cols - 1, 1) - pltpu.roll(value, 1, 1)

    height, height_1 = {}, {}
    flow_x1, flow_y1, flow_x2, flow_y2 = {}, {}, {}, {}
    height[first - 4] = load(0, first - 4)
    height[first - 3] = load(0, first - 3)
    for lead in range(first - 3, last + 7):
        row = lead
        if row < last + 3:
            height[row + 1] = load(0, row + 1)
            flow_x1[row] = inside(
                load(1, row) - GRAV * (height[row + 1] - height[row - 1]), row
            )
            if first - 2 <= row < last + 2:
                flow_y1[row] = load(2, row) - GRAV * across_y(height[row])
        row = lead - 1
        if first - 2 <= row < last + 2:
            height_1[row] = inside(
                height[row]
                - DEPTH * (flow_x1[row + 1] - flow_x1[row - 1] + across_y(flow_y1[row])),
                row,
            )
        row = lead - 2
        if first - 1 <= row < last + 1:
            flow_x2[row] = inside(
                flow_x1[row] - GRAV * (height_1[row + 1] - height_1[row - 1]), row
            )
            if first <= row < last:
                flow_y2[row] = flow_y1[row] - GRAV * across_y(height_1[row])
                store(1, row, flow_x2[row])
                store(2, row, flow_y2[row])
        row = lead - 3
        if first <= row < last:
            store(
                0,
                row,
                height_1[row]
                - DEPTH * (flow_x2[row + 1] - flow_x2[row - 1] + across_y(flow_y2[row])),
            )


def interior_kernel(dims, state_ref, out_ref):
    members, fields, rows, cols, block_rows, edge = dims
    for at in range(0, members, 8):

        def load(field, row):
            start = (at * fields + field) * rows + row
            return state_ref[pl.ds(start, 8, stride=fields * rows), :]

        def store(field, row, value):
            block, within = divmod(row, block_rows)
            out_ref[block, field * block_rows + within, at : at + 8, :] = value

        sweep(edge, rows - edge, rows, cols, load, store, lambda value, row: value)


def own_cluster(clusters):
    if clusters > DIRECT:
        return 0
    return lax.axis_index("group") * lax.axis_size("member") + lax.axis_index("member")


def edge_kernel(dims, state_ref, before_ref, after_ref, interior_ref, *refs):
    members, fields, rows, cols, block_rows, edge = dims
    clusters = rows // block_rows
    slots, edges_ref = refs[:clusters], refs[clusters]
    here = lax.axis_index("space")
    has_before = (here > 0).astype(jnp.float32)
    has_after = (here < lax.axis_size("space") - 1).astype(jnp.float32)
    own = own_cluster(clusters)

    def inside(value, row):
        if row < 0:
            return value * has_before
        if row >= rows:
            return value * has_after
        return value

    for at in range(0, members, 8):

        def load(field, row):
            offset = sum(HALO[:field])
            if row < 0:
                return before_ref[offset + HALO[field] + row, at : at + 8, :]
            if row >= rows:
                return after_ref[offset + row - rows, at : at + 8, :]
            start = (at * fields + field) * rows + row
            return state_ref[pl.ds(start, 8, stride=fields * rows), :]

        def store(field, row, value):
            block, within = divmod(row, block_rows)
            edges_ref[block, field * block_rows + within, at : at + 8, :] = value

        sweep(0, edge, rows, cols, load, store, inside)
        sweep(rows - edge, rows, rows, cols, load, store, inside)
    edges_ref[edge // block_rows : clusters - edge // block_rows] = interior_ref[
        edge // block_rows : clusters - edge // block_rows
    ]
    for slot, ref in zip(slot_order(clusters), slots):
        ref[...] = edges_ref[own ^ slot]


def forecast(state, clusters):
    members, fields, rows, cols = state.shape
    block_rows = rows // clusters
    terms = fields * block_rows
    edge = -(-4 // block_rows) * block_rows
    to_prev, to_next = pack_edges(state)
    count = lax.axis_size("space")
    before = lax.ppermute(to_next, "space", [(i, i + 1) for i in range(count - 1)])
    after = lax.ppermute(to_prev, "space", [(i + 1, i) for i in range(count - 1)])
    dims = (members, fields, rows, cols, block_rows, edge)
    flat = state.reshape(members * fields * rows, cols)
    size = members * fields * rows * cols
    interior = call(
        functools.partial(interior_kernel, dims),
        f32(clusters, terms, members, cols),
        1,
        cost_estimate=pl.CostEstimate(
            flops=200 * size, bytes_accessed=16 * size, transcendentals=0
        ),
    )(flat)
    return call(
        functools.partial(edge_kernel, dims),
        [f32(terms, members, cols)] * clusters,
        4,
        [pltpu.VMEM((clusters, terms, members, cols), jnp.float32)],
    )(flat, before, after, interior)


def slot_order(clusters):
    if clusters > DIRECT:
        return list(range(clusters))
    cores = lax.axis_size("member")
    return [0] + sorted(range(1, clusters), key=lambda s: (s < cores, s % cores, s))


def exchange(values, slots):
    clusters = lax.axis_size("group") * lax.axis_size("member")
    if clusters > DIRECT:
        stacked = jnp.stack(values, axis=0)
        got = lax.all_to_all(stacked, ("group", "member"), split_axis=0, concat_axis=0, tiled=True)
        return [got[k] for k in range(clusters)]
    return [
        lax.ppermute(value, ("group", "member"), [(i, i ^ slot) for i in range(clusters)])
        if slot
        else value
        for slot, value in zip(slots, values)
    ]


def shares():
    return (lax.axis_size("group"), lax.axis_size("member")) == (4, 2)


def term_parts(terms):
    cuts = [0, terms // 3, terms // 2, terms // 2 + terms // 3, terms] if shares() else [0, terms]
    return [range(first, last) for first, last in zip(cuts, cuts[1:])]


def pieces(slot):
    if not shares():
        return [(0, 0)]
    first, second = 2, 4
    along_first = [(0, 2), (0, 3), (second, 2), (second, 3)]
    along_second = [(0, 0), (0, 1), (first, 0), (first, 1)]
    if slot < first:
        return along_second + along_first
    if slot & first and slot & second:
        return []
    return along_first if slot & first else along_second


def return_slots(clusters):
    return [slot for slot in slot_order(clusters) if pieces(slot)]


def split(value):
    high = value.astype(jnp.bfloat16)
    rest = value - high.astype(jnp.float32)
    middle = rest.astype(jnp.bfloat16)
    low = (rest - middle.astype(jnp.float32)).astype(jnp.bfloat16)
    return high, middle, low


def observed_kernel(values_ref, precision_ref, index_ref, out_ref):
    count = index_ref.shape[1]
    width = out_ref.shape[1]
    parts = list(split(precision_ref[...])) + list(split(values_ref[...]))
    pad = jnp.zeros((16 - len(parts), count), jnp.bfloat16)
    rows = jnp.concatenate(parts + [pad], axis=0)
    position = lax.broadcasted_iota(jnp.int32, (width, count), 0)
    hit = (position == index_ref[...]).astype(jnp.float32).astype(jnp.bfloat16)
    placed = lax.dot_general(
        rows, hit, (((1,), (1,)), ((), ())), preferred_element_type=jnp.float32
    )
    out_ref[0:1, :] = placed[0:1] + placed[1:2] + placed[2:3]
    out_ref[1:2, :] = placed[3:4] + placed[4:5] + placed[5:6]
    out_ref[2:8, :] = jnp.zeros((6, width), jnp.float32)


def product(left, right, contract):
    return lax.dot_general(
        left,
        right,
        (contract, ((), ())),
        precision=lax.Precision.HIGHEST,
        preferred_element_type=jnp.float32,
    )


def gram_kernel(dims, observed_ref, *refs):
    clusters, terms, members, cols = dims
    arrived, (out_ref, *parts, scaled_ref) = refs[:clusters], refs[clusters:]
    total = clusters * members
    scale = 1.0 / math.sqrt(total - 1)
    half = LANES
    own = own_cluster(clusters)
    places = [pl.multiple_of((own ^ slot) * members, members) for slot in slot_order(clusters)]
    for term in range(terms):
        at = slice(term * cols, (term + 1) * cols)
        values = [ref[term] for ref in arrived]
        summed = values[0]
        for value in values[1:]:
            summed = summed + value
        mean = jnp.sum(summed, axis=0, keepdims=True) * (1.0 / total)
        part = [term in held for held in term_parts(terms)].index(True)
        there = term - term_parts(terms)[part].start
        there = slice(there * cols, (there + 1) * cols)
        parts[part][total : total + 8, there] = jnp.broadcast_to(mean, (8, cols))
        weight = observed_ref[0:1, at] * scale
        for place, value in zip(places, values):
            anomaly = value - mean
            parts[part][pl.ds(place, members), there] = anomaly
            scaled_ref[pl.ds(place, members), at] = anomaly * weight
        innovation = (observed_ref[1:2, at] - mean) * weight
        scaled_ref[total : total + 8, at] = jnp.concatenate(
            [innovation, jnp.zeros((7, cols), jnp.float32)], axis=0
        )
    result = short_product(scaled_ref[...], scaled_ref[0:total, :], ((1,), (1,)))
    at = 0
    for first in range(0, total, half):
        out_ref[at : at + total - first, :] = result[first:total, first : first + half]
        at += total - first
    for k, first in enumerate(range(0, total, half)):
        out_ref[at + 8 * k : at + 8 * k + 8, :] = result[total : total + 8, first : first + half]
    at += 8 * (total // half)
    if at < out_ref.shape[0]:
        out_ref[at:, :] = jnp.zeros((out_ref.shape[0] - at, half), jnp.float32)


def flip(value, axis, bits):
    return lax.ppermute(value, axis, [(i, i ^ bits) for i in range(lax.axis_size(axis))])


def total_over_devices(value, parts):
    held = {(0, k): part for k, part in enumerate(parts)}
    if not shares() or lax.axis_size("space") != 4:
        if shares():
            for k, part in enumerate(parts):
                bit = 1 + k // 2
                held[2 * bit, k] = flip(part, "group", bit)
        return lax.psum(value, ("group", "member", "space")), held
    rows, cols = value.shape
    core = lax.axis_index("member")
    chip = lax.axis_index("group")
    half = rows // 2
    part = half // 4
    kept = lax.dynamic_slice_in_dim(value, core * half, half, 0)
    given = lax.dynamic_slice_in_dim(value, (1 - core) * half, half, 0)
    summed = (kept + flip(given, "member", 1)).reshape(4, part, cols)
    pieces = [lax.dynamic_index_in_dim(summed, chip ^ s, 0, False) for s in range(4)]
    piece = pieces[0] + (
        flip(pieces[1], "group", 1) + flip(pieces[2], "group", 2) + flip(pieces[3], "group", 3)
    )
    piece, early0, early2 = lax.optimization_barrier((piece, parts[0], parts[2]))
    early0, early2 = flip(early0, "group", 1), flip(early2, "group", 2)
    piece = piece + (flip(piece, "space", 3) + flip(piece, "space", 2) + flip(piece, "space", 1))
    piece, held[2, 0], held[4, 2] = lax.optimization_barrier((piece, early0, early2))
    got = jnp.stack([piece] + [flip(piece, "group", s) for s in (1, 2, 3)], axis=0)
    mine = jnp.concatenate(
        [lax.dynamic_index_in_dim(got, chip ^ i, 0, False) for i in range(4)], axis=0
    )
    mine, late1, late3 = lax.optimization_barrier((mine, parts[1], parts[3]))
    held[2, 1], held[4, 3] = flip(late1, "group", 1), flip(late3, "group", 2)
    other = flip(mine, "member", 1)
    whole_sum = jnp.concatenate(
        [jnp.where(core == 0, mine, other), jnp.where(core == 0, other, mine)], axis=0
    )
    return whole_sum, held


def short_product(left, right, contract):
    left_high, right_high = left.astype(jnp.bfloat16), right.astype(jnp.bfloat16)
    left_low = (left - left_high.astype(jnp.float32)).astype(jnp.bfloat16)
    right_low = (right - right_high.astype(jnp.float32)).astype(jnp.bfloat16)

    def dot(x, y):
        return lax.dot_general(x, y, (contract, ((), ())), preferred_element_type=jnp.float32)

    return dot(left_high, right_high) + (dot(left_high, right_low) + dot(left_low, right_high))


def eliminate(panel, first):
    tile = 8
    size, width = panel.shape
    count = size // tile
    rows = [panel[at : at + tile, :] for at in range(0, size, tile)]
    lane = lax.broadcasted_iota(jnp.int32, (tile, width), 1)
    sublane = lax.broadcasted_iota(jnp.int32, (tile, width), 0)

    def row(value, at):
        return jnp.broadcast_to(value[at : at + 1, :], (tile, width))

    def column(value, at):
        return jnp.broadcast_to(value[:, at : at + 1], (tile, width))

    ahead = None
    for own in range(count):
        start = first + own * tile
        columns = [[column(value, start + k) for k in range(tile)] for value in rows[own:]]
        if ahead is not None:
            columns[0] = ahead
        if own + 1 < count:
            for value, spread in zip(rows[own : own + 2], columns):
                spread += [column(value, start + k) for k in range(tile, 2 * tile)]
        pivots = (lane >= start) & (lane < start + tile)
        cleared = [jnp.where(pivots, 0.0, value) for value in rows[own:]]
        local = columns[0]
        right = jnp.where(lane - start == sublane, 1.0, cleared[0])
        done = right
        solved = []
        for p in range(0, tile, 2):
            s00, s10, s11 = row(local[p], p), row(local[p], p + 1), row(local[p + 1], p + 1)
            inv0 = 1.0 / s00
            inv1 = s00 * (1.0 / (s00 * s11 - s10 * s10))
            low = s10 * inv0
            upper = []
            for k in range(p + 2, len(local)):
                u0 = row(local[k], p)
                upper.append((u0 * inv0, (row(local[k], p + 1) - low * u0) * inv1))
            r0 = row(right, p)
            r1 = row(right, p + 1) - low * r0
            solved += [r0 * inv0, r1 * inv1]
            done = jnp.where(sublane == p, r0 * lax.rsqrt(s00), done)
            done = jnp.where(sublane == p + 1, r1 * (inv1 * lax.rsqrt(inv1)), done)
            for value in columns:
                value[p + 1] = value[p + 1] - low * value[p]
                for k, (u0, u1) in zip(range(p + 2, len(value)), upper):
                    value[k] = value[k] - (value[p] * u0 + value[p + 1] * u1)
            if p + 2 < tile:
                right = right - (local[p] * solved[p] + local[p + 1] * solved[p + 1])
        rows[own] = jnp.where((lane - start > sublane) & (lane < first + size), 0.0, done)
        if own + 1 < count:
            ahead = columns[1][tile:]
        for k in range(own + 1, count):
            terms = [left * value for left, value in zip(columns[k - own], solved)]
            while len(terms) > 1:
                terms = [x + y for x, y in zip(terms[::2], terms[1::2])]
            rows[k] = cleared[k - own] - terms[0]
    return jnp.concatenate(rows, axis=0)


def inverse_factor(block, panel=64):
    size = block.shape[0]
    done = []
    rest = block
    for first in range(0, size, panel):
        rows = eliminate(rest[:panel], first)
        lane = lax.broadcasted_iota(jnp.int32, rows.shape, 1)
        done.append(jnp.where(lane < first + panel, rows, 0.0))
        if first + panel < size:
            rest = rest[panel:]
            lane = lax.broadcasted_iota(jnp.int32, rest.shape, 1)
            pivots = (lane >= first) & (lane < first + panel)
            change = product(rows, rows, ((0,), (0,)))
            rest = jnp.where(pivots, 0.0, rest) - change[first + panel :]
    return jnp.concatenate(done, axis=0)


def transform_of(packed_ref, total):
    half = LANES
    count = total // half
    ROWS, LAST = ((1,), (0,)), ((1,), (1,))
    gram, at = {}, 0
    for column in range(count):
        for row in range(column, count):
            gram[row, column] = packed_ref[at : at + half, :]
            at += half
    pull = [packed_ref[at + 8 * k : at + 8 * k + 1, :] for k in range(count)]
    diagonal = lax.broadcasted_iota(jnp.int32, (half, half), 0) == lax.broadcasted_iota(
        jnp.int32, (half, half), 1
    )
    identity = jnp.where(diagonal, 1.0, 0.0)
    factor, inverse = {}, {}
    for column in range(count):
        for row in range(column, count):
            left = gram[row, column]
            if row == column:
                left = left + identity
            for k in range(column):
                left = left - product(factor[row, k], factor[column, k], LAST)
            if row == column:
                inverse[row, row] = inverse_factor(left)
            else:
                factor[row, column] = product(left, inverse[column, column], LAST)
    for row in range(count):
        for column in range(row):
            total_term = product(factor[row, column], inverse[column, column], ROWS)
            for k in range(column + 1, row):
                total_term = total_term + product(factor[row, k], inverse[k, column], ROWS)
            inverse[row, column] = -product(inverse[row, row], total_term, ROWS)
    inner = [
        sum(
            jnp.sum(inverse[row, column] * pull[column], axis=1, keepdims=True)
            for column in range(row + 1)
        )
        for row in range(count)
    ]
    weights = [
        sum(
            jnp.sum(inverse[row, column] * inner[row], axis=0, keepdims=True)
            for row in range(column, count)
        )
        for column in range(count)
    ]
    zero = jnp.zeros((half, half), jnp.float32)
    return jnp.concatenate(
        [
            jnp.concatenate(
                [inverse.get((row, column), zero) + weights[column] for column in range(count)],
                axis=1,
            )
            for row in range(count)
        ],
        axis=0,
    )


def transform_kernel(total, packed_ref, out_ref):
    out_ref[...] = transform_of(packed_ref, total)


def update_kernel(dims, sources, transform_ref, *refs):
    clusters, terms, members, cols = dims
    slots = return_slots(clusters)
    out = dict(zip(slots, refs[len(sources) :]))
    total = clusters * members
    own = own_cluster(clusters)
    for (source, part), ref in zip(sources, refs):
        targets = [slot for slot in slots if (source, part) in pieces(slot)]
        transform = jnp.concatenate(
            [
                transform_ref[pl.ds(pl.multiple_of((own ^ slot) * members, members), members), :]
                for slot in targets
            ],
            axis=0,
        )
        updated = short_product(transform, ref[0:total, :], ((1,), (0,))) + ref[total : total + 1, :]
        for place, slot in enumerate(targets):
            held = pieces(slot)
            first = sum(len(term_parts(terms)[k]) for _, k in held[: held.index((source, part))])
            for term in range(len(term_parts(terms)[part])):
                out[slot][first + term] = updated[
                    place * members : (place + 1) * members, term * cols : (term + 1) * cols
                ]


def place_kernel(dims, *refs):
    clusters, fields, block_rows, cols = dims
    out_ref = refs[-1]
    rows = clusters * block_rows
    own = own_cluster(clusters)
    for slot, ref in zip(return_slots(clusters), refs):
        held = 0
        for source, part in pieces(slot):
            first = (own ^ (slot ^ source)) * block_rows
            for term in term_parts(fields * block_rows)[part]:
                field, row = divmod(term, block_rows)
                at = field * rows + row + first
                out_ref[pl.ds(at, 8, stride=fields * rows), :] = ref[held]
                held += 1


def place(values, clusters, fields, terms):
    _, members, cols = values[0].shape
    rows = clusters * terms
    return pl.pallas_call(
        functools.partial(place_kernel, (clusters, fields, terms // fields, cols)),
        grid=(members // 8,),
        out_shape=f32(members * rows, cols),
        in_specs=[pl.BlockSpec((value.shape[0], 8, cols), lambda i: (0, i, 0)) for value in values],
        out_specs=pl.BlockSpec((8 * rows, cols), lambda i: (i, 0)),
        compiler_params=pltpu.CompilerParams(vmem_limit_bytes=VMEM_LIMIT),
    )(*values)


def on_device(state, obs_values, obs_precision, obs_index):
    members, fields, rows, cols = state.shape
    clusters = lax.axis_size("group") * lax.axis_size("member")
    terms = fields * (rows // clusters)
    total = clusters * members
    width = terms * cols
    dims = (clusters, terms, members, cols)
    sizes = [len(part) for part in term_parts(terms)]
    arrived = exchange(forecast(state, clusters), slot_order(clusters))
    observed = call(observed_kernel, f32(8, width), 3)(obs_values, obs_precision, obs_index)
    packed, *parts = call(
        functools.partial(gram_kernel, dims),
        [f32(448, LANES)] + [f32(total + 8, size * cols) for size in sizes],
        1 + clusters,
        [pltpu.VMEM((total + 8, width), jnp.float32)],
    )(observed, *arrived)
    packed, held = total_over_devices(packed, parts)
    transform = call(functools.partial(transform_kernel, total), f32(total, total), 1)(packed)
    slots = return_slots(clusters)
    sources = sorted({piece for slot in slots for piece in pieces(slot)})
    updated = call(
        functools.partial(update_kernel, dims, sources),
        [f32(sum(sizes[part] for _, part in pieces(slot)), members, cols) for slot in slots],
        1 + len(sources),
    )(transform, *[held[source] for source in sources])
    returned = exchange(updated, slots)
    return place(returned, clusters, fields, terms).reshape(members, fields, rows, cols)


def solution(mesh):
    blocks = P(("group", "member", "space"), None)
    state = P(("group", "member"), None, "space", None)
    return jax.shard_map(
        on_device,
        mesh=mesh,
        in_specs=(state, blocks, blocks, blocks),
        out_specs=state,
        check_vma=False,
    )
```

```python
import functools
import math

import jax
import jax.numpy as jnp
from jax import lax
from jax.experimental import pallas as pl
from jax.experimental.pallas import tpu as pltpu
from jax.sharding import PartitionSpec as P

STEPS = 2
GRAV = 0.4
DEPTH = 0.4
HALO = (4, 3, 2)
HALO_ROWS = sum(HALO)
LANES = 128
DIRECT = 8
VMEM_LIMIT = 40 * 1024 * 1024


def whole(shape, memory_space=pltpu.VMEM):
    return pl.BlockSpec(memory_space=memory_space)


def call(kernel, out_shape, n_in, scratch=(), **kw):
    single = not isinstance(out_shape, (list, tuple))
    n_out = 1 if single else len(out_shape)
    spec = pl.BlockSpec(memory_space=pltpu.VMEM)
    return pl.pallas_call(
        kernel,
        out_shape=out_shape,
        in_specs=[spec] * n_in,
        out_specs=spec if single else [spec] * n_out,
        scratch_shapes=list(scratch),
        compiler_params=pltpu.CompilerParams(vmem_limit_bytes=VMEM_LIMIT),
        **kw,
    )


def f32(*shape):
    return jax.ShapeDtypeStruct(shape, jnp.float32)


def pack_kernel(top_ref, bottom_ref, outer_ref, inner_ref):
    edge = top_ref.shape[2]
    even = lax.rem(lax.axis_index("space"), 2) == 0
    at = 0
    for field, rows in enumerate(HALO):
        for row in range(rows):
            to_prev = top_ref[:, field, row, :]
            to_next = bottom_ref[:, field, edge - rows + row, :]
            outer_ref[at] = jnp.where(even, to_prev, to_next)
            inner_ref[at] = jnp.where(even, to_next, to_prev)
            at += 1


def pack_edges(state):
    members, fields, rows, cols = state.shape
    edge = 8
    last = rows // edge - 1
    block = (members, fields, edge, cols)
    out = f32(HALO_ROWS, members, cols)
    out_spec = pl.BlockSpec((HALO_ROWS, members, cols), lambda i: (0, 0, 0))
    return pl.pallas_call(
        pack_kernel,
        grid=(1,),
        out_shape=[out, out],
        in_specs=[
            pl.BlockSpec(block, lambda i: (0, 0, 0, 0)),
            pl.BlockSpec(block, lambda i: (0, 0, last, 0)),
        ],
        out_specs=[out_spec, out_spec],
        compiler_params=pltpu.CompilerParams(vmem_limit_bytes=VMEM_LIMIT),
    )(state, state)


def sweep(first, last, rows, cols, load, store, inside):
    def across_y(value):
        return pltpu.roll(value, cols - 1, 1) - pltpu.roll(value, 1, 1)

    height, height_1 = {}, {}
    flow_x1, flow_y1, flow_x2, flow_y2 = {}, {}, {}, {}
    height[first - 4] = load(0, first - 4)
    height[first - 3] = load(0, first - 3)
    for lead in range(first - 3, last + 7):
        row = lead
        if row < last + 3:
            height[row + 1] = load(0, row + 1)
            flow_x1[row] = inside(
                load(1, row) - GRAV * (height[row + 1] - height[row - 1]), row
            )
            if first - 2 <= row < last + 2:
                flow_y1[row] = load(2, row) - GRAV * across_y(height[row])
        row = lead - 1
        if first - 2 <= row < last + 2:
            height_1[row] = inside(
                height[row]
                - DEPTH * (flow_x1[row + 1] - flow_x1[row - 1] + across_y(flow_y1[row])),
                row,
            )
        row = lead - 2
        if first - 1 <= row < last + 1:
            flow_x2[row] = inside(
                flow_x1[row] - GRAV * (height_1[row + 1] - height_1[row - 1]), row
            )
            if first <= row < last:
                flow_y2[row] = flow_y1[row] - GRAV * across_y(height_1[row])
                store(1, row, flow_x2[row])
                store(2, row, flow_y2[row])
        row = lead - 3
        if first <= row < last:
            store(
                0,
                row,
                height_1[row]
                - DEPTH * (flow_x2[row + 1] - flow_x2[row - 1] + across_y(flow_y2[row])),
            )


def interior_kernel(dims, state_ref, out_ref):
    members, fields, rows, cols, block_rows, edge = dims
    for at in range(0, members, 8):

        def load(field, row):
            start = (at * fields + field) * rows + row
            return state_ref[pl.ds(start, 8, stride=fields * rows), :]

        def store(field, row, value):
            block, within = divmod(row, block_rows)
            out_ref[block, field * block_rows + within, at : at + 8, :] = value

        sweep(edge, rows - edge, rows, cols, load, store, lambda value, row: value)


def own_cluster(clusters):
    if clusters > DIRECT:
        return 0
    return lax.axis_index("group") * lax.axis_size("member") + lax.axis_index("member")


def edge_kernel(dims, state_ref, outer_ref, inner_ref, interior_ref, *refs):
    members, fields, rows, cols, block_rows, edge = dims
    clusters = rows // block_rows
    slots, edges_ref = refs[:clusters], refs[clusters]
    here = lax.axis_index("space")
    even = lax.rem(here, 2) == 0
    has_before = (here > 0).astype(jnp.float32)
    has_after = (here < lax.axis_size("space") - 1).astype(jnp.float32)
    own = own_cluster(clusters)

    def inside(value, row):
        if row < 0:
            return value * has_before
        if row >= rows:
            return value * has_after
        return value

    for at in range(0, members, 8):

        def load(field, row):
            offset = sum(HALO[:field])
            if row < 0:
                held = offset + HALO[field] + row
                outer, inner = outer_ref[held, at : at + 8, :], inner_ref[held, at : at + 8, :]
                return jnp.where(even, outer, inner)
            if row >= rows:
                held = offset + row - rows
                outer, inner = outer_ref[held, at : at + 8, :], inner_ref[held, at : at + 8, :]
                return jnp.where(even, inner, outer)
            start = (at * fields + field) * rows + row
            return state_ref[pl.ds(start, 8, stride=fields * rows), :]

        def store(field, row, value):
            block, within = divmod(row, block_rows)
            edges_ref[block, field * block_rows + within, at : at + 8, :] = value

        sweep(0, edge, rows, cols, load, store, inside)
        sweep(rows - edge, rows, rows, cols, load, store, inside)
    edges_ref[edge // block_rows : clusters - edge // block_rows] = interior_ref[
        edge // block_rows : clusters - edge // block_rows
    ]
    for slot, ref in zip(slot_order(clusters), slots):
        ref[...] = edges_ref[own ^ slot]


def forecast(state, clusters):
    members, fields, rows, cols = state.shape
    block_rows = rows // clusters
    terms = fields * block_rows
    edge = -(-4 // block_rows) * block_rows
    outer, inner = pack_edges(state)
    count = lax.axis_size("space")

    def trade(value, first):
        pairs = [(i, i + 1) for i in range(first, count - 1, 2)]
        return lax.ppermute(value, "space", pairs + [(j, i) for i, j in pairs])

    outer, inner = trade(outer, 1), trade(inner, 0)
    dims = (members, fields, rows, cols, block_rows, edge)
    flat = state.reshape(members * fields * rows, cols)
    size = members * fields * rows * cols
    interior = call(
        functools.partial(interior_kernel, dims),
        f32(clusters, terms, members, cols),
        1,
        cost_estimate=pl.CostEstimate(
            flops=200 * size, bytes_accessed=16 * size, transcendentals=0
        ),
    )(flat)
    return call(
        functools.partial(edge_kernel, dims),
        [f32(terms, members, cols)] * clusters,
        4,
        [pltpu.VMEM((clusters, terms, members, cols), jnp.float32)],
    )(flat, outer, inner, interior)


def slot_order(clusters):
    if clusters > DIRECT:
        return list(range(clusters))
    cores = lax.axis_size("member")
    return [0] + sorted(range(1, clusters), key=lambda s: (s < cores, s % cores, s))


def exchange(values, slots):
    clusters = lax.axis_size("group") * lax.axis_size("member")
    if clusters > DIRECT:
        stacked = jnp.stack(values, axis=0)
        got = lax.all_to_all(stacked, ("group", "member"), split_axis=0, concat_axis=0, tiled=True)
        return [got[k] for k in range(clusters)]
    return [
        lax.ppermute(value, ("group", "member"), [(i, i ^ slot) for i in range(clusters)])
        if slot
        else value
        for slot, value in zip(slots, values)
    ]


def shares():
    return (lax.axis_size("group"), lax.axis_size("member")) == (4, 2)


def term_parts(terms):
    cuts = [0, terms // 3, terms // 2, terms // 2 + terms // 3, terms] if shares() else [0, terms]
    return [range(first, last) for first, last in zip(cuts, cuts[1:])]


def pieces(slot):
    if not shares():
        return [(0, 0)]
    first, second = 2, 4
    along_first = [(0, 2), (0, 3), (second, 2), (second, 3)]
    along_second = [(0, 0), (0, 1), (first, 0), (first, 1)]
    if slot < first:
        return along_second + along_first
    if slot & first and slot & second:
        return []
    return along_first if slot & first else along_second


def return_slots(clusters):
    return [slot for slot in slot_order(clusters) if pieces(slot)]


def split(value):
    high = value.astype(jnp.bfloat16)
    rest = value - high.astype(jnp.float32)
    middle = rest.astype(jnp.bfloat16)
    low = (rest - middle.astype(jnp.float32)).astype(jnp.bfloat16)
    return high, middle, low


def observed_kernel(values_ref, precision_ref, index_ref, out_ref):
    count = index_ref.shape[1]
    width = out_ref.shape[1]
    parts = list(split(precision_ref[...])) + list(split(values_ref[...]))
    pad = jnp.zeros((16 - len(parts), count), jnp.bfloat16)
    rows = jnp.concatenate(parts + [pad], axis=0)
    position = lax.broadcasted_iota(jnp.int32, (width, count), 0)
    hit = (position == index_ref[...]).astype(jnp.float32).astype(jnp.bfloat16)
    placed = lax.dot_general(
        rows, hit, (((1,), (1,)), ((), ())), preferred_element_type=jnp.float32
    )
    out_ref[0:1, :] = placed[0:1] + placed[1:2] + placed[2:3]
    out_ref[1:2, :] = placed[3:4] + placed[4:5] + placed[5:6]
    out_ref[2:8, :] = jnp.zeros((6, width), jnp.float32)


def product(left, right, contract):
    return lax.dot_general(
        left,
        right,
        (contract, ((), ())),
        precision=lax.Precision.HIGHEST,
        preferred_element_type=jnp.float32,
    )


def gram_kernel(dims, observed_ref, *refs):
    clusters, terms, members, cols = dims
    arrived, (out_ref, *parts, scaled_ref) = refs[:clusters], refs[clusters:]
    total = clusters * members
    scale = 1.0 / math.sqrt(total - 1)
    half = LANES
    own = own_cluster(clusters)
    places = [pl.multiple_of((own ^ slot) * members, members) for slot in slot_order(clusters)]
    for term in range(terms):
        at = slice(term * cols, (term + 1) * cols)
        values = [ref[term] for ref in arrived]
        summed = values[0]
        for value in values[1:]:
            summed = summed + value
        mean = jnp.sum(summed, axis=0, keepdims=True) * (1.0 / total)
        part = [term in held for held in term_parts(terms)].index(True)
        there = term - term_parts(terms)[part].start
        there = slice(there * cols, (there + 1) * cols)
        parts[part][total : total + 8, there] = jnp.broadcast_to(mean, (8, cols))
        weight = observed_ref[0:1, at] * scale
        for place, value in zip(places, values):
            anomaly = value - mean
            parts[part][pl.ds(place, members), there] = anomaly
            scaled_ref[pl.ds(place, members), at] = anomaly * weight
        innovation = (observed_ref[1:2, at] - mean) * weight
        scaled_ref[total : total + 8, at] = jnp.concatenate(
            [innovation, jnp.zeros((7, cols), jnp.float32)], axis=0
        )
    result = short_product(scaled_ref[...], scaled_ref[0:total, :], ((1,), (1,)))
    at = 0
    for first in range(0, total, half):
        out_ref[at : at + total - first, :] = result[first:total, first : first + half]
        at += total - first
    for k, first in enumerate(range(0, total, half)):
        out_ref[at + 8 * k : at + 8 * k + 8, :] = result[total : total + 8, first : first + half]
    at += 8 * (total // half)
    if at < out_ref.shape[0]:
        out_ref[at:, :] = jnp.zeros((out_ref.shape[0] - at, half), jnp.float32)


def flip(value, axis, bits):
    return lax.ppermute(value, axis, [(i, i ^ bits) for i in range(lax.axis_size(axis))])


def total_over_devices(value, parts):
    held = {(0, k): part for k, part in enumerate(parts)}
    if not shares() or lax.axis_size("space") != 4:
        if shares():
            for k, part in enumerate(parts):
                bit = 1 + k // 2
                held[2 * bit, k] = flip(part, "group", bit)
        return lax.psum(value, ("group", "member", "space")), held
    rows, cols = value.shape
    core = lax.axis_index("member")
    chip = lax.axis_index("group")
    half = rows // 2
    part = half // 4
    kept = lax.dynamic_slice_in_dim(value, core * half, half, 0)
    given = lax.dynamic_slice_in_dim(value, (1 - core) * half, half, 0)
    summed = (kept + flip(given, "member", 1)).reshape(4, part, cols)
    pieces = [lax.dynamic_index_in_dim(summed, chip ^ s, 0, False) for s in range(4)]
    piece = pieces[0] + (
        flip(pieces[1], "group", 1) + flip(pieces[2], "group", 2) + flip(pieces[3], "group", 3)
    )
    piece, early0, early2 = lax.optimization_barrier((piece, parts[0], parts[2]))
    early0, early2 = flip(early0, "group", 1), flip(early2, "group", 2)
    piece = piece + (flip(piece, "space", 3) + flip(piece, "space", 2) + flip(piece, "space", 1))
    piece, held[2, 0], held[4, 2] = lax.optimization_barrier((piece, early0, early2))
    got = jnp.stack([piece] + [flip(piece, "group", s) for s in (1, 2, 3)], axis=0)
    mine = jnp.concatenate(
        [lax.dynamic_index_in_dim(got, chip ^ i, 0, False) for i in range(4)], axis=0
    )
    mine, late1, late3 = lax.optimization_barrier((mine, parts[1], parts[3]))
    held[2, 1], held[4, 3] = flip(late1, "group", 1), flip(late3, "group", 2)
    other = flip(mine, "member", 1)
    whole_sum = jnp.concatenate(
        [jnp.where(core == 0, mine, other), jnp.where(core == 0, other, mine)], axis=0
    )
    return whole_sum, held


def short_product(left, right, contract):
    left_high, right_high = left.astype(jnp.bfloat16), right.astype(jnp.bfloat16)
    left_low = (left - left_high.astype(jnp.float32)).astype(jnp.bfloat16)
    right_low = (right - right_high.astype(jnp.float32)).astype(jnp.bfloat16)

    def dot(x, y):
        return lax.dot_general(x, y, (contract, ((), ())), preferred_element_type=jnp.float32)

    return dot(left_high, right_high) + (dot(left_high, right_low) + dot(left_low, right_high))


def eliminate(panel, first):
    tile = 8
    size, width = panel.shape
    count = size // tile
    rows = [panel[at : at + tile, :] for at in range(0, size, tile)]
    lane = lax.broadcasted_iota(jnp.int32, (tile, width), 1)
    sublane = lax.broadcasted_iota(jnp.int32, (tile, width), 0)

    def row(value, at):
        return jnp.broadcast_to(value[at : at + 1, :], (tile, width))

    def column(value, at):
        return jnp.broadcast_to(value[:, at : at + 1], (tile, width))

    ahead = None
    for own in range(count):
        start = first + own * tile
        columns = [[column(value, start + k) for k in range(tile)] for value in rows[own:]]
        if ahead is not None:
            columns[0] = ahead
        if own + 1 < count:
            for value, spread in zip(rows[own : own + 2], columns):
                spread += [column(value, start + k) for k in range(tile, 2 * tile)]
        pivots = (lane >= start) & (lane < start + tile)
        cleared = [jnp.where(pivots, 0.0, value) for value in rows[own:]]
        local = columns[0]
        right = jnp.where(lane - start == sublane, 1.0, cleared[0])
        done = right
        solved = []
        for p in range(0, tile, 2):
            s00, s10, s11 = row(local[p], p), row(local[p], p + 1), row(local[p + 1], p + 1)
            inv0 = 1.0 / s00
            inv1 = s00 * (1.0 / (s00 * s11 - s10 * s10))
            low = s10 * inv0
            upper = []
            for k in range(p + 2, len(local)):
                u0 = row(local[k], p)
                upper.append((u0 * inv0, (row(local[k], p + 1) - low * u0) * inv1))
            r0 = row(right, p)
            r1 = row(right, p + 1) - low * r0
            solved += [r0 * inv0, r1 * inv1]
            done = jnp.where(sublane == p, r0 * lax.rsqrt(s00), done)
            done = jnp.where(sublane == p + 1, r1 * (inv1 * lax.rsqrt(inv1)), done)
            for value in columns:
                value[p + 1] = value[p + 1] - low * value[p]
                for k, (u0, u1) in zip(range(p + 2, len(value)), upper):
                    value[k] = value[k] - (value[p] * u0 + value[p + 1] * u1)
            if p + 2 < tile:
                right = right - (local[p] * solved[p] + local[p + 1] * solved[p + 1])
        rows[own] = jnp.where((lane - start > sublane) & (lane < first + size), 0.0, done)
        if own + 1 < count:
            ahead = columns[1][tile:]
        for k in range(own + 1, count):
            terms = [left * value for left, value in zip(columns[k - own], solved)]
            while len(terms) > 1:
                terms = [x + y for x, y in zip(terms[::2], terms[1::2])]
            rows[k] = cleared[k - own] - terms[0]
    return jnp.concatenate(rows, axis=0)


def inverse_factor(block, panel=64):
    size = block.shape[0]
    done = []
    rest = block
    for first in range(0, size, panel):
        rows = eliminate(rest[:panel], first)
        lane = lax.broadcasted_iota(jnp.int32, rows.shape, 1)
        done.append(jnp.where(lane < first + panel, rows, 0.0))
        if first + panel < size:
            rest = rest[panel:]
            lane = lax.broadcasted_iota(jnp.int32, rest.shape, 1)
            pivots = (lane >= first) & (lane < first + panel)
            change = product(rows, rows, ((0,), (0,)))
            rest = jnp.where(pivots, 0.0, rest) - change[first + panel :]
    return jnp.concatenate(done, axis=0)


def transform_of(packed_ref, total):
    half = LANES
    count = total // half
    ROWS, LAST = ((1,), (0,)), ((1,), (1,))
    gram, at = {}, 0
    for column in range(count):
        for row in range(column, count):
            gram[row, column] = packed_ref[at : at + half, :]
            at += half
    pull = [packed_ref[at + 8 * k : at + 8 * k + 1, :] for k in range(count)]
    diagonal = lax.broadcasted_iota(jnp.int32, (half, half), 0) == lax.broadcasted_iota(
        jnp.int32, (half, half), 1
    )
    identity = jnp.where(diagonal, 1.0, 0.0)
    factor, inverse = {}, {}
    for column in range(count):
        for row in range(column, count):
            left = gram[row, column]
            if row == column:
                left = left + identity
            for k in range(column):
                left = left - product(factor[row, k], factor[column, k], LAST)
            if row == column:
                inverse[row, row] = inverse_factor(left)
            else:
                factor[row, column] = product(left, inverse[column, column], LAST)
    for row in range(count):
        for column in range(row):
            total_term = product(factor[row, column], inverse[column, column], ROWS)
            for k in range(column + 1, row):
                total_term = total_term + product(factor[row, k], inverse[k, column], ROWS)
            inverse[row, column] = -product(inverse[row, row], total_term, ROWS)
    inner = [
        sum(
            jnp.sum(inverse[row, column] * pull[column], axis=1, keepdims=True)
            for column in range(row + 1)
        )
        for row in range(count)
    ]
    weights = [
        sum(
            jnp.sum(inverse[row, column] * inner[row], axis=0, keepdims=True)
            for row in range(column, count)
        )
        for column in range(count)
    ]
    zero = jnp.zeros((half, half), jnp.float32)
    return jnp.concatenate(
        [
            jnp.concatenate(
                [inverse.get((row, column), zero) + weights[column] for column in range(count)],
                axis=1,
            )
            for row in range(count)
        ],
        axis=0,
    )


def transform_kernel(total, packed_ref, out_ref):
    out_ref[...] = transform_of(packed_ref, total)


def update_kernel(dims, sources, transform_ref, *refs):
    clusters, terms, members, cols = dims
    slots = return_slots(clusters)
    out = dict(zip(slots, refs[len(sources) :]))
    total = clusters * members
    own = own_cluster(clusters)
    for (source, part), ref in zip(sources, refs):
        targets = [slot for slot in slots if (source, part) in pieces(slot)]
        transform = jnp.concatenate(
            [
                transform_ref[pl.ds(pl.multiple_of((own ^ slot) * members, members), members), :]
                for slot in targets
            ],
            axis=0,
        )
        updated = short_product(transform, ref[0:total, :], ((1,), (0,))) + ref[total : total + 1, :]
        for place, slot in enumerate(targets):
            held = pieces(slot)
            first = sum(len(term_parts(terms)[k]) for _, k in held[: held.index((source, part))])
            for term in range(len(term_parts(terms)[part])):
                out[slot][first + term] = updated[
                    place * members : (place + 1) * members, term * cols : (term + 1) * cols
                ]


def place_kernel(dims, *refs):
    clusters, fields, block_rows, members, cols, groups = dims
    slots = return_slots(clusters)
    values, (out_ref, placed_ref, sent) = refs[: len(slots)], refs[len(slots) :]
    rows = clusters * block_rows
    own = own_cluster(clusters)
    size = members // groups
    copies = []
    for group in range(groups):
        for slot, ref in zip(slots, values):
            held = 0
            for source, part in pieces(slot):
                first = (own ^ (slot ^ source)) * block_rows
                for term in term_parts(fields * block_rows)[part]:
                    field, row = divmod(term, block_rows)
                    at = group * size * fields * rows + field * rows + row + first
                    placed_ref[pl.ds(at, size, stride=fields * rows), :] = ref[
                        held, group * size : (group + 1) * size, :
                    ]
                    held += 1
        span = pl.ds(group * size * fields * rows, size * fields * rows)
        copies.append(pltpu.make_async_copy(placed_ref.at[span], out_ref.at[span], sent.at[group]))
        copies[-1].start()
    for copy in copies:
        copy.wait()


def place(values, clusters, fields, terms):
    _, members, cols = values[0].shape
    rows = clusters * terms
    groups = members // 8
    spec = pl.BlockSpec(memory_space=pltpu.VMEM)
    return pl.pallas_call(
        functools.partial(
            place_kernel, (clusters, fields, terms // fields, members, cols, groups)
        ),
        out_shape=f32(members * rows, cols),
        in_specs=[spec] * len(values),
        out_specs=pl.BlockSpec(memory_space=pl.ANY),
        scratch_shapes=[
            pltpu.VMEM((members * rows, cols), jnp.float32),
            pltpu.SemaphoreType.DMA((groups,)),
        ],
        compiler_params=pltpu.CompilerParams(vmem_limit_bytes=VMEM_LIMIT),
    )(*values)


def on_device(state, obs_values, obs_precision, obs_index):
    members, fields, rows, cols = state.shape
    clusters = lax.axis_size("group") * lax.axis_size("member")
    terms = fields * (rows // clusters)
    total = clusters * members
    width = terms * cols
    dims = (clusters, terms, members, cols)
    sizes = [len(part) for part in term_parts(terms)]
    arrived = exchange(forecast(state, clusters), slot_order(clusters))
    observed = call(observed_kernel, f32(8, width), 3)(obs_values, obs_precision, obs_index)
    packed, *parts = call(
        functools.partial(gram_kernel, dims),
        [f32(448, LANES)] + [f32(total + 8, size * cols) for size in sizes],
        1 + clusters,
        [pltpu.VMEM((total + 8, width), jnp.float32)],
    )(observed, *arrived)
    packed, held = total_over_devices(packed, parts)
    transform = call(functools.partial(transform_kernel, total), f32(total, total), 1)(packed)
    slots = return_slots(clusters)
    sources = sorted({piece for slot in slots for piece in pieces(slot)})
    updated = call(
        functools.partial(update_kernel, dims, sources),
        [f32(sum(sizes[part] for _, part in pieces(slot)), members, cols) for slot in slots],
        1 + len(sources),
    )(transform, *[held[source] for source in sources])
    returned = exchange(updated, slots)
    return place(returned, clusters, fields, terms).reshape(members, fields, rows, cols)


def solution(mesh):
    blocks = P(("group", "member", "space"), None)
    state = P(("group", "member"), None, "space", None)
    return jax.shard_map(
        on_device,
        mesh=mesh,
        in_specs=(state, blocks, blocks, blocks),
        out_specs=state,
        check_vma=False,
    )
```

```python
import functools
import math

import jax
import jax.numpy as jnp
from jax import lax
from jax.experimental import pallas as pl
from jax.experimental.pallas import tpu as pltpu
from jax.sharding import PartitionSpec as P

STEPS = 2
GRAV = 0.4
DEPTH = 0.4
HALO = (4, 3, 2)
HALO_ROWS = sum(HALO)
LANES = 128
DIRECT = 8
GROUP = 32
VMEM_LIMIT = 40 * 1024 * 1024


def whole(shape, memory_space=pltpu.VMEM):
    return pl.BlockSpec(memory_space=memory_space)


def call(kernel, out_shape, n_in, scratch=(), **kw):
    single = not isinstance(out_shape, (list, tuple))
    n_out = 1 if single else len(out_shape)
    spec = pl.BlockSpec(memory_space=pltpu.VMEM)
    return pl.pallas_call(
        kernel,
        out_shape=out_shape,
        in_specs=[spec] * n_in,
        out_specs=spec if single else [spec] * n_out,
        scratch_shapes=list(scratch),
        compiler_params=pltpu.CompilerParams(vmem_limit_bytes=VMEM_LIMIT),
        **kw,
    )


def f32(*shape):
    return jax.ShapeDtypeStruct(shape, jnp.float32)


def pack_kernel(top_ref, bottom_ref, outer_ref, inner_ref):
    edge = top_ref.shape[2]
    even = lax.rem(lax.axis_index("space"), 2) == 0
    at = 0
    for field, rows in enumerate(HALO):
        for row in range(rows):
            to_prev = top_ref[:, field, row, :]
            to_next = bottom_ref[:, field, edge - rows + row, :]
            outer_ref[at] = jnp.where(even, to_prev, to_next)
            inner_ref[at] = jnp.where(even, to_next, to_prev)
            at += 1


def pack_edges(state):
    members, fields, rows, cols = state.shape
    edge = 8
    last = rows // edge - 1
    block = (members, fields, edge, cols)
    out = f32(HALO_ROWS, members, cols)
    out_spec = pl.BlockSpec((HALO_ROWS, members, cols), lambda i: (0, 0, 0))
    return pl.pallas_call(
        pack_kernel,
        grid=(1,),
        out_shape=[out, out],
        in_specs=[
            pl.BlockSpec(block, lambda i: (0, 0, 0, 0)),
            pl.BlockSpec(block, lambda i: (0, 0, last, 0)),
        ],
        out_specs=[out_spec, out_spec],
        compiler_params=pltpu.CompilerParams(vmem_limit_bytes=VMEM_LIMIT),
    )(state, state)


def sweep(first, last, rows, cols, load, store, inside):
    def across_y(value):
        return pltpu.roll(value, cols - 1, 1) - pltpu.roll(value, 1, 1)

    height, height_1 = {}, {}
    flow_x1, flow_y1, flow_x2, flow_y2 = {}, {}, {}, {}
    height[first - 4] = load(0, first - 4)
    height[first - 3] = load(0, first - 3)
    for lead in range(first - 3, last + 7):
        row = lead
        if row < last + 3:
            height[row + 1] = load(0, row + 1)
            flow_x1[row] = inside(
                load(1, row) - GRAV * (height[row + 1] - height[row - 1]), row
            )
            if first - 2 <= row < last + 2:
                flow_y1[row] = load(2, row) - GRAV * across_y(height[row])
        row = lead - 1
        if first - 2 <= row < last + 2:
            height_1[row] = inside(
                height[row]
                - DEPTH * (flow_x1[row + 1] - flow_x1[row - 1] + across_y(flow_y1[row])),
                row,
            )
        row = lead - 2
        if first - 1 <= row < last + 1:
            flow_x2[row] = inside(
                flow_x1[row] - GRAV * (height_1[row + 1] - height_1[row - 1]), row
            )
            if first <= row < last:
                flow_y2[row] = flow_y1[row] - GRAV * across_y(height_1[row])
                store(1, row, flow_x2[row])
                store(2, row, flow_y2[row])
        row = lead - 3
        if first <= row < last:
            store(
                0,
                row,
                height_1[row]
                - DEPTH * (flow_x2[row + 1] - flow_x2[row - 1] + across_y(flow_y2[row])),
            )


def interior_kernel(dims, state_ref, out_ref):
    members, fields, rows, cols, block_rows, edge = dims
    group = min(members, GROUP)
    for at in range(0, members, group):

        def load(field, row):
            start = (at * fields + field) * rows + row
            return state_ref[pl.ds(start, group, stride=fields * rows), :]

        def store(field, row, value):
            block, within = divmod(row, block_rows)
            out_ref[block, field * block_rows + within, at : at + group, :] = value

        sweep(edge, rows - edge, rows, cols, load, store, lambda value, row: value)


def own_cluster(clusters):
    if clusters > DIRECT:
        return 0
    return lax.axis_index("group") * lax.axis_size("member") + lax.axis_index("member")


def edge_kernel(dims, state_ref, outer_ref, inner_ref, interior_ref, *refs):
    members, fields, rows, cols, block_rows, edge = dims
    group = min(members, GROUP)
    clusters = rows // block_rows
    slots, edges_ref = refs[:clusters], refs[clusters]
    here = lax.axis_index("space")
    even = lax.rem(here, 2) == 0
    has_before = (here > 0).astype(jnp.float32)
    has_after = (here < lax.axis_size("space") - 1).astype(jnp.float32)
    own = own_cluster(clusters)

    def inside(value, row):
        if row < 0:
            return value * has_before
        if row >= rows:
            return value * has_after
        return value

    for at in range(0, members, group):

        def load(field, row):
            offset = sum(HALO[:field])
            if row < 0:
                held = offset + HALO[field] + row
                outer, inner = outer_ref[held, at : at + group, :], inner_ref[held, at : at + group, :]
                return jnp.where(even, outer, inner)
            if row >= rows:
                held = offset + row - rows
                outer, inner = outer_ref[held, at : at + group, :], inner_ref[held, at : at + group, :]
                return jnp.where(even, inner, outer)
            start = (at * fields + field) * rows + row
            return state_ref[pl.ds(start, group, stride=fields * rows), :]

        def store(field, row, value):
            block, within = divmod(row, block_rows)
            edges_ref[block, field * block_rows + within, at : at + group, :] = value

        sweep(0, edge, rows, cols, load, store, inside)
        sweep(rows - edge, rows, rows, cols, load, store, inside)
    edges_ref[edge // block_rows : clusters - edge // block_rows] = interior_ref[
        edge // block_rows : clusters - edge // block_rows
    ]
    for slot, ref in zip(slot_order(clusters), slots):
        ref[...] = edges_ref[own ^ slot]


def forecast(state, clusters):
    members, fields, rows, cols = state.shape
    block_rows = rows // clusters
    terms = fields * block_rows
    edge = -(-4 // block_rows) * block_rows
    outer, inner = pack_edges(state)
    count = lax.axis_size("space")

    def trade(value, first):
        pairs = [(i, i + 1) for i in range(first, count - 1, 2)]
        return lax.ppermute(value, "space", pairs + [(j, i) for i, j in pairs])

    outer, inner = trade(outer, 1), trade(inner, 0)
    dims = (members, fields, rows, cols, block_rows, edge)
    flat = state.reshape(members * fields * rows, cols)
    size = members * fields * rows * cols
    interior = call(
        functools.partial(interior_kernel, dims),
        f32(clusters, terms, members, cols),
        1,
        cost_estimate=pl.CostEstimate(
            flops=200 * size, bytes_accessed=16 * size, transcendentals=0
        ),
    )(flat)
    return call(
        functools.partial(edge_kernel, dims),
        [f32(terms, members, cols)] * clusters,
        4,
        [pltpu.VMEM((clusters, terms, members, cols), jnp.float32)],
    )(flat, outer, inner, interior)


def slot_order(clusters):
    if clusters > DIRECT:
        return list(range(clusters))
    cores = lax.axis_size("member")
    return [0] + sorted(range(1, clusters), key=lambda s: (s < cores, s % cores, s))


def exchange(values, slots):
    clusters = lax.axis_size("group") * lax.axis_size("member")
    if clusters > DIRECT:
        stacked = jnp.stack(values, axis=0)
        got = lax.all_to_all(stacked, ("group", "member"), split_axis=0, concat_axis=0, tiled=True)
        return [got[k] for k in range(clusters)]
    return [
        lax.ppermute(value, ("group", "member"), [(i, i ^ slot) for i in range(clusters)])
        if slot
        else value
        for slot, value in zip(slots, values)
    ]


def shares():
    return (lax.axis_size("group"), lax.axis_size("member")) == (4, 2)


def term_parts(terms):
    cuts = [0, terms // 3, terms // 2, terms // 2 + terms // 3, terms] if shares() else [0, terms]
    return [range(first, last) for first, last in zip(cuts, cuts[1:])]


def pieces(slot):
    if not shares():
        return [(0, 0)]
    first, second = 2, 4
    along_first = [(0, 2), (0, 3), (second, 2), (second, 3)]
    along_second = [(0, 0), (0, 1), (first, 0), (first, 1)]
    if slot < first:
        return along_second + along_first
    if slot & first and slot & second:
        return []
    return along_first if slot & first else along_second


def return_slots(clusters):
    return [slot for slot in slot_order(clusters) if pieces(slot)]


def split(value):
    high = value.astype(jnp.bfloat16)
    rest = value - high.astype(jnp.float32)
    middle = rest.astype(jnp.bfloat16)
    low = (rest - middle.astype(jnp.float32)).astype(jnp.bfloat16)
    return high, middle, low


def observed_kernel(values_ref, precision_ref, index_ref, out_ref):
    count = index_ref.shape[1]
    width = out_ref.shape[1]
    parts = list(split(precision_ref[...])) + list(split(values_ref[...]))
    pad = jnp.zeros((16 - len(parts), count), jnp.bfloat16)
    rows = jnp.concatenate(parts + [pad], axis=0)
    position = lax.broadcasted_iota(jnp.int32, (width, count), 0)
    hit = (position == index_ref[...]).astype(jnp.float32).astype(jnp.bfloat16)
    placed = lax.dot_general(
        rows, hit, (((1,), (1,)), ((), ())), preferred_element_type=jnp.float32
    )
    out_ref[0:1, :] = placed[0:1] + placed[1:2] + placed[2:3]
    out_ref[1:2, :] = placed[3:4] + placed[4:5] + placed[5:6]
    out_ref[2:8, :] = jnp.zeros((6, width), jnp.float32)


def product(left, right, contract):
    return lax.dot_general(
        left,
        right,
        (contract, ((), ())),
        precision=lax.Precision.HIGHEST,
        preferred_element_type=jnp.float32,
    )


def gram_kernel(dims, observed_ref, *refs):
    clusters, terms, members, cols = dims
    arrived, (out_ref, *parts, scaled_ref) = refs[:clusters], refs[clusters:]
    total = clusters * members
    scale = 1.0 / math.sqrt(total - 1)
    half = LANES
    own = own_cluster(clusters)
    places = [pl.multiple_of((own ^ slot) * members, members) for slot in slot_order(clusters)]
    for term in range(terms):
        at = slice(term * cols, (term + 1) * cols)
        values = [ref[term] for ref in arrived]
        summed = values[0]
        for value in values[1:]:
            summed = summed + value
        mean = jnp.sum(summed, axis=0, keepdims=True) * (1.0 / total)
        part = [term in held for held in term_parts(terms)].index(True)
        there = term - term_parts(terms)[part].start
        there = slice(there * cols, (there + 1) * cols)
        parts[part][total : total + 8, there] = jnp.broadcast_to(mean, (8, cols))
        weight = observed_ref[0:1, at] * scale
        for place, value in zip(places, values):
            anomaly = value - mean
            parts[part][pl.ds(place, members), there] = anomaly
            scaled_ref[pl.ds(place, members), at] = anomaly * weight
        innovation = (observed_ref[1:2, at] - mean) * weight
        scaled_ref[total : total + 8, at] = jnp.concatenate(
            [innovation, jnp.zeros((7, cols), jnp.float32)], axis=0
        )
    result = short_product(scaled_ref[...], scaled_ref[0:total, :], ((1,), (1,)))
    at = 0
    for first in range(0, total, half):
        out_ref[at : at + total - first, :] = result[first:total, first : first + half]
        at += total - first
    for k, first in enumerate(range(0, total, half)):
        out_ref[at + 8 * k : at + 8 * k + 8, :] = result[total : total + 8, first : first + half]
    at += 8 * (total // half)
    if at < out_ref.shape[0]:
        out_ref[at:, :] = jnp.zeros((out_ref.shape[0] - at, half), jnp.float32)


def flip(value, axis, bits):
    return lax.ppermute(value, axis, [(i, i ^ bits) for i in range(lax.axis_size(axis))])


def total_over_devices(value, parts):
    held = {(0, k): part for k, part in enumerate(parts)}
    if not shares() or lax.axis_size("space") != 4:
        if shares():
            for k, part in enumerate(parts):
                bit = 1 + k // 2
                held[2 * bit, k] = flip(part, "group", bit)
        return lax.psum(value, ("group", "member", "space")), held
    rows, cols = value.shape
    core = lax.axis_index("member")
    chip = lax.axis_index("group")
    half = rows // 2
    part = half // 4
    kept = lax.dynamic_slice_in_dim(value, core * half, half, 0)
    given = lax.dynamic_slice_in_dim(value, (1 - core) * half, half, 0)
    summed = (kept + flip(given, "member", 1)).reshape(4, part, cols)
    pieces = [lax.dynamic_index_in_dim(summed, chip ^ s, 0, False) for s in range(4)]
    piece = pieces[0] + (
        flip(pieces[1], "group", 1) + flip(pieces[2], "group", 2) + flip(pieces[3], "group", 3)
    )
    piece, early0, early2 = lax.optimization_barrier((piece, parts[0], parts[2]))
    early0, early2 = flip(early0, "group", 1), flip(early2, "group", 2)
    piece = piece + (flip(piece, "space", 3) + flip(piece, "space", 2) + flip(piece, "space", 1))
    piece, held[2, 0], held[4, 2] = lax.optimization_barrier((piece, early0, early2))
    got = jnp.stack([piece] + [flip(piece, "group", s) for s in (1, 2, 3)], axis=0)
    mine = jnp.concatenate(
        [lax.dynamic_index_in_dim(got, chip ^ i, 0, False) for i in range(4)], axis=0
    )
    mine, late1, late3 = lax.optimization_barrier((mine, parts[1], parts[3]))
    held[2, 1], held[4, 3] = flip(late1, "group", 1), flip(late3, "group", 2)
    other = flip(mine, "member", 1)
    whole_sum = jnp.concatenate(
        [jnp.where(core == 0, mine, other), jnp.where(core == 0, other, mine)], axis=0
    )
    return whole_sum, held


def short_product(left, right, contract):
    left_high, right_high = left.astype(jnp.bfloat16), right.astype(jnp.bfloat16)
    left_low = (left - left_high.astype(jnp.float32)).astype(jnp.bfloat16)
    right_low = (right - right_high.astype(jnp.float32)).astype(jnp.bfloat16)

    def dot(x, y):
        return lax.dot_general(x, y, (contract, ((), ())), preferred_element_type=jnp.float32)

    return dot(left_high, right_high) + (dot(left_high, right_low) + dot(left_low, right_high))


def eliminate(panel, first):
    tile = 8
    size, width = panel.shape
    count = size // tile
    rows = [panel[at : at + tile, :] for at in range(0, size, tile)]
    lane = lax.broadcasted_iota(jnp.int32, (tile, width), 1)
    sublane = lax.broadcasted_iota(jnp.int32, (tile, width), 0)

    def row(value, at):
        return jnp.broadcast_to(value[at : at + 1, :], (tile, width))

    def column(value, at):
        return jnp.broadcast_to(value[:, at : at + 1], (tile, width))

    ahead = None
    for own in range(count):
        start = first + own * tile
        columns = [[column(value, start + k) for k in range(tile)] for value in rows[own:]]
        if ahead is not None:
            columns[0] = ahead
        if own + 1 < count:
            for value, spread in zip(rows[own : own + 2], columns):
                spread += [column(value, start + k) for k in range(tile, 2 * tile)]
        pivots = (lane >= start) & (lane < start + tile)
        cleared = [jnp.where(pivots, 0.0, value) for value in rows[own:]]
        local = columns[0]
        right = jnp.where(lane - start == sublane, 1.0, cleared[0])
        done = right
        solved = []
        for p in range(0, tile, 2):
            s00, s10, s11 = row(local[p], p), row(local[p], p + 1), row(local[p + 1], p + 1)
            inv0 = 1.0 / s00
            inv1 = s00 * (1.0 / (s00 * s11 - s10 * s10))
            low = s10 * inv0
            upper = []
            for k in range(p + 2, len(local)):
                u0 = row(local[k], p)
                upper.append((u0 * inv0, (row(local[k], p + 1) - low * u0) * inv1))
            r0 = row(right, p)
            r1 = row(right, p + 1) - low * r0
            solved += [r0 * inv0, r1 * inv1]
            done = jnp.where(sublane == p, r0 * lax.rsqrt(s00), done)
            done = jnp.where(sublane == p + 1, r1 * (inv1 * lax.rsqrt(inv1)), done)
            for value in columns:
                value[p + 1] = value[p + 1] - low * value[p]
                for k, (u0, u1) in zip(range(p + 2, len(value)), upper):
                    value[k] = value[k] - (value[p] * u0 + value[p + 1] * u1)
            if p + 2 < tile:
                right = right - (local[p] * solved[p] + local[p + 1] * solved[p + 1])
        rows[own] = jnp.where((lane - start > sublane) & (lane < first + size), 0.0, done)
        if own + 1 < count:
            ahead = columns[1][tile:]
        for k in range(own + 1, count):
            terms = [left * value for left, value in zip(columns[k - own], solved)]
            while len(terms) > 1:
                terms = [x + y for x, y in zip(terms[::2], terms[1::2])]
            rows[k] = cleared[k - own] - terms[0]
    return jnp.concatenate(rows, axis=0)


def inverse_factor(block, panel=64):
    size = block.shape[0]
    done = []
    rest = block
    for first in range(0, size, panel):
        rows = eliminate(rest[:panel], first)
        lane = lax.broadcasted_iota(jnp.int32, rows.shape, 1)
        done.append(jnp.where(lane < first + panel, rows, 0.0))
        if first + panel < size:
            rest = rest[panel:]
            lane = lax.broadcasted_iota(jnp.int32, rest.shape, 1)
            pivots = (lane >= first) & (lane < first + panel)
            change = product(rows, rows, ((0,), (0,)))
            rest = jnp.where(pivots, 0.0, rest) - change[first + panel :]
    return jnp.concatenate(done, axis=0)


def transform_of(packed_ref, total):
    half = LANES
    count = total // half
    ROWS, LAST = ((1,), (0,)), ((1,), (1,))
    gram, at = {}, 0
    for column in range(count):
        for row in range(column, count):
            gram[row, column] = packed_ref[at : at + half, :]
            at += half
    pull = [packed_ref[at + 8 * k : at + 8 * k + 1, :] for k in range(count)]
    diagonal = lax.broadcasted_iota(jnp.int32, (half, half), 0) == lax.broadcasted_iota(
        jnp.int32, (half, half), 1
    )
    identity = jnp.where(diagonal, 1.0, 0.0)
    factor, inverse = {}, {}
    for column in range(count):
        for row in range(column, count):
            left = gram[row, column]
            if row == column:
                left = left + identity
            for k in range(column):
                left = left - product(factor[row, k], factor[column, k], LAST)
            if row == column:
                inverse[row, row] = inverse_factor(left)
            else:
                factor[row, column] = product(left, inverse[column, column], LAST)
    for row in range(count):
        for column in range(row):
            total_term = product(factor[row, column], inverse[column, column], ROWS)
            for k in range(column + 1, row):
                total_term = total_term + product(factor[row, k], inverse[k, column], ROWS)
            inverse[row, column] = -product(inverse[row, row], total_term, ROWS)
    inner = [
        sum(
            jnp.sum(inverse[row, column] * pull[column], axis=1, keepdims=True)
            for column in range(row + 1)
        )
        for row in range(count)
    ]
    weights = [
        sum(
            jnp.sum(inverse[row, column] * inner[row], axis=0, keepdims=True)
            for row in range(column, count)
        )
        for column in range(count)
    ]
    zero = jnp.zeros((half, half), jnp.float32)
    return jnp.concatenate(
        [
            jnp.concatenate(
                [inverse.get((row, column), zero) + weights[column] for column in range(count)],
                axis=1,
            )
            for row in range(count)
        ],
        axis=0,
    )


def transform_kernel(total, packed_ref, out_ref):
    out_ref[...] = transform_of(packed_ref, total)


def update_kernel(dims, sources, transform_ref, *refs):
    clusters, terms, members, cols = dims
    slots = return_slots(clusters)
    out = dict(zip(slots, refs[len(sources) :]))
    total = clusters * members
    own = own_cluster(clusters)
    for (source, part), ref in zip(sources, refs):
        targets = [slot for slot in slots if (source, part) in pieces(slot)]
        transform = jnp.concatenate(
            [
                transform_ref[pl.ds(pl.multiple_of((own ^ slot) * members, members), members), :]
                for slot in targets
            ],
            axis=0,
        )
        updated = short_product(transform, ref[0:total, :], ((1,), (0,))) + ref[total : total + 1, :]
        for place, slot in enumerate(targets):
            held = pieces(slot)
            first = sum(len(term_parts(terms)[k]) for _, k in held[: held.index((source, part))])
            for term in range(len(term_parts(terms)[part])):
                out[slot][first + term] = updated[
                    place * members : (place + 1) * members, term * cols : (term + 1) * cols
                ]


def place_kernel(dims, *refs):
    clusters, fields, block_rows, members, cols, groups = dims
    slots = return_slots(clusters)
    values, (out_ref, placed_ref, sent) = refs[: len(slots)], refs[len(slots) :]
    rows = clusters * block_rows
    own = own_cluster(clusters)
    size = members // groups
    copies = []
    for group in range(groups):
        for slot, ref in zip(slots, values):
            held = 0
            for source, part in pieces(slot):
                first = (own ^ (slot ^ source)) * block_rows
                for term in term_parts(fields * block_rows)[part]:
                    field, row = divmod(term, block_rows)
                    at = group * size * fields * rows + field * rows + row + first
                    placed_ref[pl.ds(at, size, stride=fields * rows), :] = ref[
                        held, group * size : (group + 1) * size, :
                    ]
                    held += 1
        span = pl.ds(group * size * fields * rows, size * fields * rows)
        copies.append(pltpu.make_async_copy(placed_ref.at[span], out_ref.at[span], sent.at[group]))
        copies[-1].start()
    for copy in copies:
        copy.wait()


def place(values, clusters, fields, terms):
    _, members, cols = values[0].shape
    rows = clusters * terms
    groups = members // 8
    spec = pl.BlockSpec(memory_space=pltpu.VMEM)
    return pl.pallas_call(
        functools.partial(
            place_kernel, (clusters, fields, terms // fields, members, cols, groups)
        ),
        out_shape=f32(members * rows, cols),
        in_specs=[spec] * len(values),
        out_specs=pl.BlockSpec(memory_space=pl.ANY),
        scratch_shapes=[
            pltpu.VMEM((members * rows, cols), jnp.float32),
            pltpu.SemaphoreType.DMA((groups,)),
        ],
        compiler_params=pltpu.CompilerParams(vmem_limit_bytes=VMEM_LIMIT),
    )(*values)


def on_device(state, obs_values, obs_precision, obs_index):
    members, fields, rows, cols = state.shape
    clusters = lax.axis_size("group") * lax.axis_size("member")
    terms = fields * (rows // clusters)
    total = clusters * members
    width = terms * cols
    dims = (clusters, terms, members, cols)
    sizes = [len(part) for part in term_parts(terms)]
    arrived = exchange(forecast(state, clusters), slot_order(clusters))
    observed = call(observed_kernel, f32(8, width), 3)(obs_values, obs_precision, obs_index)
    packed, *parts = call(
        functools.partial(gram_kernel, dims),
        [f32(448, LANES)] + [f32(total + 8, size * cols) for size in sizes],
        1 + clusters,
        [pltpu.VMEM((total + 8, width), jnp.float32)],
    )(observed, *arrived)
    packed, held = total_over_devices(packed, parts)
    transform = call(functools.partial(transform_kernel, total), f32(total, total), 1)(packed)
    slots = return_slots(clusters)
    sources = sorted({piece for slot in slots for piece in pieces(slot)})
    updated = call(
        functools.partial(update_kernel, dims, sources),
        [f32(sum(sizes[part] for _, part in pieces(slot)), members, cols) for slot in slots],
        1 + len(sources),
    )(transform, *[held[source] for source in sources])
    returned = exchange(updated, slots)
    return place(returned, clusters, fields, terms).reshape(members, fields, rows, cols)


def solution(mesh):
    blocks = P(("group", "member", "space"), None)
    state = P(("group", "member"), None, "space", None)
    return jax.shard_map(
        on_device,
        mesh=mesh,
        in_specs=(state, blocks, blocks, blocks),
        out_specs=state,
        check_vma=False,
    )
```

```python
import functools
import math

import jax
import jax.numpy as jnp
from jax import lax
from jax.experimental import pallas as pl
from jax.experimental.pallas import tpu as pltpu
from jax.sharding import PartitionSpec as P

STEPS = 2
GRAV = 0.4
DEPTH = 0.4
HALO = (4, 3, 2)
HALO_ROWS = sum(HALO)
LANES = 128
DIRECT = 8
GROUP = 32
VMEM_LIMIT = 40 * 1024 * 1024


def whole(shape, memory_space=pltpu.VMEM):
    return pl.BlockSpec(memory_space=memory_space)


def call(kernel, out_shape, n_in, scratch=(), **kw):
    single = not isinstance(out_shape, (list, tuple))
    n_out = 1 if single else len(out_shape)
    spec = pl.BlockSpec(memory_space=pltpu.VMEM)
    return pl.pallas_call(
        kernel,
        out_shape=out_shape,
        in_specs=[spec] * n_in,
        out_specs=spec if single else [spec] * n_out,
        scratch_shapes=list(scratch),
        compiler_params=pltpu.CompilerParams(vmem_limit_bytes=VMEM_LIMIT),
        **kw,
    )


def f32(*shape):
    return jax.ShapeDtypeStruct(shape, jnp.float32)


def pack_kernel(top_ref, bottom_ref, outer_ref, inner_ref):
    edge = top_ref.shape[2]
    even = lax.rem(lax.axis_index("space"), 2) == 0
    at = 0
    for field, rows in enumerate(HALO):
        for row in range(rows):
            to_prev = top_ref[:, field, row, :]
            to_next = bottom_ref[:, field, edge - rows + row, :]
            outer_ref[at] = jnp.where(even, to_prev, to_next)
            inner_ref[at] = jnp.where(even, to_next, to_prev)
            at += 1


def pack_edges(state):
    members, fields, rows, cols = state.shape
    edge = 8
    last = rows // edge - 1
    block = (members, fields, edge, cols)
    out = f32(HALO_ROWS, members, cols)
    out_spec = pl.BlockSpec((HALO_ROWS, members, cols), lambda i: (0, 0, 0))
    return pl.pallas_call(
        pack_kernel,
        grid=(1,),
        out_shape=[out, out],
        in_specs=[
            pl.BlockSpec(block, lambda i: (0, 0, 0, 0)),
            pl.BlockSpec(block, lambda i: (0, 0, last, 0)),
        ],
        out_specs=[out_spec, out_spec],
        compiler_params=pltpu.CompilerParams(vmem_limit_bytes=VMEM_LIMIT),
    )(state, state)


def sweep(first, last, rows, cols, load, store, inside):
    def across_y(value):
        return pltpu.roll(value, cols - 1, 1) - pltpu.roll(value, 1, 1)

    height, height_1 = {}, {}
    flow_x1, flow_y1, flow_x2, flow_y2 = {}, {}, {}, {}
    height[first - 4] = load(0, first - 4)
    height[first - 3] = load(0, first - 3)
    for lead in range(first - 3, last + 7):
        row = lead
        if row < last + 3:
            height[row + 1] = load(0, row + 1)
            flow_x1[row] = inside(
                load(1, row) - GRAV * (height[row + 1] - height[row - 1]), row
            )
            if first - 2 <= row < last + 2:
                flow_y1[row] = load(2, row) - GRAV * across_y(height[row])
        row = lead - 1
        if first - 2 <= row < last + 2:
            height_1[row] = inside(
                height[row]
                - DEPTH * (flow_x1[row + 1] - flow_x1[row - 1] + across_y(flow_y1[row])),
                row,
            )
        row = lead - 2
        if first - 1 <= row < last + 1:
            flow_x2[row] = inside(
                flow_x1[row] - GRAV * (height_1[row + 1] - height_1[row - 1]), row
            )
            if first <= row < last:
                flow_y2[row] = flow_y1[row] - GRAV * across_y(height_1[row])
                store(1, row, flow_x2[row])
                store(2, row, flow_y2[row])
        row = lead - 3
        if first <= row < last:
            store(
                0,
                row,
                height_1[row]
                - DEPTH * (flow_x2[row + 1] - flow_x2[row - 1] + across_y(flow_y2[row])),
            )


def interior_kernel(dims, state_ref, out_ref):
    members, fields, rows, cols, block_rows, edge = dims
    group = min(members, GROUP)
    for at in range(0, members, group):

        def load(field, row):
            start = (at * fields + field) * rows + row
            return state_ref[pl.ds(start, group, stride=fields * rows), :]

        def store(field, row, value):
            block, within = divmod(row, block_rows)
            out_ref[block, field * block_rows + within, at : at + group, :] = value

        sweep(edge, rows - edge, rows, cols, load, store, lambda value, row: value)


def own_cluster(clusters):
    if clusters > DIRECT:
        return 0
    return lax.axis_index("group") * lax.axis_size("member") + lax.axis_index("member")


def edge_kernel(dims, state_ref, outer_ref, inner_ref, interior_ref, *refs):
    members, fields, rows, cols, block_rows, edge = dims
    group = min(members, GROUP)
    clusters = rows // block_rows
    slots, edges_ref = refs[:clusters], refs[clusters]
    here = lax.axis_index("space")
    even = lax.rem(here, 2) == 0
    has_before = (here > 0).astype(jnp.float32)
    has_after = (here < lax.axis_size("space") - 1).astype(jnp.float32)
    own = own_cluster(clusters)

    def inside(value, row):
        if row < 0:
            return value * has_before
        if row >= rows:
            return value * has_after
        return value

    for at in range(0, members, group):

        def load(field, row):
            offset = sum(HALO[:field])
            if row < 0:
                held = offset + HALO[field] + row
                outer, inner = outer_ref[held, at : at + group, :], inner_ref[held, at : at + group, :]
                return jnp.where(even, outer, inner)
            if row >= rows:
                held = offset + row - rows
                outer, inner = outer_ref[held, at : at + group, :], inner_ref[held, at : at + group, :]
                return jnp.where(even, inner, outer)
            start = (at * fields + field) * rows + row
            return state_ref[pl.ds(start, group, stride=fields * rows), :]

        def store(field, row, value):
            block, within = divmod(row, block_rows)
            edges_ref[block, field * block_rows + within, at : at + group, :] = value

        sweep(0, edge, rows, cols, load, store, inside)
        sweep(rows - edge, rows, rows, cols, load, store, inside)
    edges_ref[edge // block_rows : clusters - edge // block_rows] = interior_ref[
        edge // block_rows : clusters - edge // block_rows
    ]
    for slot, ref in zip(slot_order(clusters), slots):
        ref[...] = edges_ref[own ^ slot]


def forecast(state, clusters):
    members, fields, rows, cols = state.shape
    block_rows = rows // clusters
    terms = fields * block_rows
    edge = -(-4 // block_rows) * block_rows
    outer, inner = pack_edges(state)
    count = lax.axis_size("space")

    def trade(value, first):
        pairs = [(i, i + 1) for i in range(first, count - 1, 2)]
        return lax.ppermute(value, "space", pairs + [(j, i) for i, j in pairs])

    outer, inner = trade(outer, 1), trade(inner, 0)
    dims = (members, fields, rows, cols, block_rows, edge)
    flat = state.reshape(members * fields * rows, cols)
    size = members * fields * rows * cols
    interior = call(
        functools.partial(interior_kernel, dims),
        f32(clusters, terms, members, cols),
        1,
        cost_estimate=pl.CostEstimate(
            flops=200 * size, bytes_accessed=16 * size, transcendentals=0
        ),
    )(flat)
    return call(
        functools.partial(edge_kernel, dims),
        [f32(terms, members, cols)] * clusters,
        4,
        [pltpu.VMEM((clusters, terms, members, cols), jnp.float32)],
    )(flat, outer, inner, interior)


def slot_order(clusters):
    if clusters > DIRECT:
        return list(range(clusters))
    cores = lax.axis_size("member")
    return [0] + sorted(range(1, clusters), key=lambda s: (s < cores, s % cores, s))


def exchange(values, slots):
    clusters = lax.axis_size("group") * lax.axis_size("member")
    if clusters > DIRECT:
        stacked = jnp.stack(values, axis=0)
        got = lax.all_to_all(stacked, ("group", "member"), split_axis=0, concat_axis=0, tiled=True)
        return [got[k] for k in range(clusters)]
    return [
        lax.ppermute(value, ("group", "member"), [(i, i ^ slot) for i in range(clusters)])
        if slot
        else value
        for slot, value in zip(slots, values)
    ]


def shares():
    return (lax.axis_size("group"), lax.axis_size("member")) == (4, 2)


def term_parts(terms):
    cuts = [0, terms // 3, terms // 2, terms // 2 + terms // 3, terms] if shares() else [0, terms]
    return [range(first, last) for first, last in zip(cuts, cuts[1:])]


def pieces(slot):
    if not shares():
        return [(0, 0)]
    first, second = 2, 4
    along_first = [(0, 2), (0, 3), (second, 2), (second, 3)]
    along_second = [(0, 0), (0, 1), (first, 0), (first, 1)]
    if slot < first:
        return along_second + along_first
    if slot & first and slot & second:
        return []
    return along_first if slot & first else along_second


def return_slots(clusters):
    return [slot for slot in slot_order(clusters) if pieces(slot)]


def split(value):
    high = value.astype(jnp.bfloat16)
    rest = value - high.astype(jnp.float32)
    middle = rest.astype(jnp.bfloat16)
    low = (rest - middle.astype(jnp.float32)).astype(jnp.bfloat16)
    return high, middle, low


def observed_kernel(values_ref, precision_ref, index_ref, out_ref):
    count = index_ref.shape[1]
    width = out_ref.shape[1]
    parts = list(split(precision_ref[...])) + list(split(values_ref[...]))
    pad = jnp.zeros((16 - len(parts), count), jnp.bfloat16)
    rows = jnp.concatenate(parts + [pad], axis=0)
    position = lax.broadcasted_iota(jnp.int32, (width, count), 0)
    hit = (position == index_ref[...]).astype(jnp.float32).astype(jnp.bfloat16)
    placed = lax.dot_general(
        rows, hit, (((1,), (1,)), ((), ())), preferred_element_type=jnp.float32
    )
    out_ref[0:1, :] = placed[0:1] + placed[1:2] + placed[2:3]
    out_ref[1:2, :] = placed[3:4] + placed[4:5] + placed[5:6]
    out_ref[2:8, :] = jnp.zeros((6, width), jnp.float32)


def product(left, right, contract):
    return lax.dot_general(
        left,
        right,
        (contract, ((), ())),
        precision=lax.Precision.HIGHEST,
        preferred_element_type=jnp.float32,
    )


def gram_kernel(dims, observed_ref, *refs):
    clusters, terms, members, cols = dims
    arrived, (out_ref, *parts, scaled_ref) = refs[:clusters], refs[clusters:]
    total = clusters * members
    scale = 1.0 / math.sqrt(total - 1)
    half = LANES
    own = own_cluster(clusters)
    places = [pl.multiple_of((own ^ slot) * members, members) for slot in slot_order(clusters)]
    for term in range(terms):
        at = slice(term * cols, (term + 1) * cols)
        values = [ref[term] for ref in arrived]
        summed = values[0]
        for value in values[1:]:
            summed = summed + value
        mean = jnp.sum(summed, axis=0, keepdims=True) * (1.0 / total)
        part = [term in held for held in term_parts(terms)].index(True)
        there = term - term_parts(terms)[part].start
        there = slice(there * cols, (there + 1) * cols)
        parts[part][total : total + 8, there] = jnp.broadcast_to(mean, (8, cols))
        weight = observed_ref[0:1, at] * scale
        for place, value in zip(places, values):
            anomaly = value - mean
            parts[part][pl.ds(place, members), there] = anomaly
            scaled_ref[pl.ds(place, members), at] = anomaly * weight
        innovation = (observed_ref[1:2, at] - mean) * weight
        scaled_ref[total : total + 8, at] = jnp.concatenate(
            [innovation, jnp.zeros((7, cols), jnp.float32)], axis=0
        )
    result = short_product(scaled_ref[...], scaled_ref[0:total, :], ((1,), (1,)), low_terms=True)
    at = 0
    for first in range(0, total, half):
        out_ref[at : at + total - first, :] = result[first:total, first : first + half]
        at += total - first
    for k, first in enumerate(range(0, total, half)):
        out_ref[at + 8 * k : at + 8 * k + 8, :] = result[total : total + 8, first : first + half]
    at += 8 * (total // half)
    if at < out_ref.shape[0]:
        out_ref[at:, :] = jnp.zeros((out_ref.shape[0] - at, half), jnp.float32)


def flip(value, axis, bits):
    return lax.ppermute(value, axis, [(i, i ^ bits) for i in range(lax.axis_size(axis))])


def total_over_devices(value, parts):
    held = {(0, k): part for k, part in enumerate(parts)}
    if not shares() or lax.axis_size("space") != 4:
        if shares():
            for k, part in enumerate(parts):
                bit = 1 + k // 2
                held[2 * bit, k] = flip(part, "group", bit)
        return lax.psum(value, ("group", "member", "space")), held
    rows, cols = value.shape
    core = lax.axis_index("member")
    chip = lax.axis_index("group")
    half = rows // 2
    part = half // 4
    kept = lax.dynamic_slice_in_dim(value, core * half, half, 0)
    given = lax.dynamic_slice_in_dim(value, (1 - core) * half, half, 0)
    summed = (kept + flip(given, "member", 1)).reshape(4, part, cols)
    pieces = [lax.dynamic_index_in_dim(summed, chip ^ s, 0, False) for s in range(4)]
    piece = pieces[0] + (
        flip(pieces[1], "group", 1) + flip(pieces[2], "group", 2) + flip(pieces[3], "group", 3)
    )
    piece, early0, early2 = lax.optimization_barrier((piece, parts[0], parts[2]))
    early0, early2 = flip(early0, "group", 1), flip(early2, "group", 2)
    piece = piece + (flip(piece, "space", 3) + flip(piece, "space", 2) + flip(piece, "space", 1))
    piece, held[2, 0], held[4, 2] = lax.optimization_barrier((piece, early0, early2))
    got = jnp.stack([piece] + [flip(piece, "group", s) for s in (1, 2, 3)], axis=0)
    mine = jnp.concatenate(
        [lax.dynamic_index_in_dim(got, chip ^ i, 0, False) for i in range(4)], axis=0
    )
    mine, late1, late3 = lax.optimization_barrier((mine, parts[1], parts[3]))
    held[2, 1], held[4, 3] = flip(late1, "group", 1), flip(late3, "group", 2)
    other = flip(mine, "member", 1)
    whole_sum = jnp.concatenate(
        [jnp.where(core == 0, mine, other), jnp.where(core == 0, other, mine)], axis=0
    )
    return whole_sum, held


def short_product(left, right, contract, low_terms=False):
    left_high, right_high = left.astype(jnp.bfloat16), right.astype(jnp.bfloat16)
    left_low = (left - left_high.astype(jnp.float32)).astype(jnp.bfloat16)
    right_low = (right - right_high.astype(jnp.float32)).astype(jnp.bfloat16)

    def dot(x, y):
        return lax.dot_general(x, y, (contract, ((), ())), preferred_element_type=jnp.float32)

    small = dot(left_high, right_low) + dot(left_low, right_high)
    if low_terms:
        small = small + dot(left_low, right_low)
    return dot(left_high, right_high) + small


def eliminate(panel, first):
    tile = 8
    size, width = panel.shape
    count = size // tile
    rows = [panel[at : at + tile, :] for at in range(0, size, tile)]
    lane = lax.broadcasted_iota(jnp.int32, (tile, width), 1)
    sublane = lax.broadcasted_iota(jnp.int32, (tile, width), 0)

    def row(value, at):
        return jnp.broadcast_to(value[at : at + 1, :], (tile, width))

    def column(value, at):
        return jnp.broadcast_to(value[:, at : at + 1], (tile, width))

    ahead = None
    for own in range(count):
        start = first + own * tile
        columns = [[column(value, start + k) for k in range(tile)] for value in rows[own:]]
        if ahead is not None:
            columns[0] = ahead
        if own + 1 < count:
            for value, spread in zip(rows[own : own + 2], columns):
                spread += [column(value, start + k) for k in range(tile, 2 * tile)]
        pivots = (lane >= start) & (lane < start + tile)
        cleared = [jnp.where(pivots, 0.0, value) for value in rows[own:]]
        local = columns[0]
        right = jnp.where(lane - start == sublane, 1.0, cleared[0])
        done = right
        solved = []
        for p in range(0, tile, 2):
            s00, s10, s11 = row(local[p], p), row(local[p], p + 1), row(local[p + 1], p + 1)
            inv0 = 1.0 / s00
            inv1 = s00 * (1.0 / (s00 * s11 - s10 * s10))
            low = s10 * inv0
            upper = []
            for k in range(p + 2, len(local)):
                u0 = row(local[k], p)
                upper.append((u0 * inv0, (row(local[k], p + 1) - low * u0) * inv1))
            r0 = row(right, p)
            r1 = row(right, p + 1) - low * r0
            solved += [r0 * inv0, r1 * inv1]
            done = jnp.where(sublane == p, r0 * lax.rsqrt(s00), done)
            done = jnp.where(sublane == p + 1, r1 * (inv1 * lax.rsqrt(inv1)), done)
            for value in columns:
                value[p + 1] = value[p + 1] - low * value[p]
                for k, (u0, u1) in zip(range(p + 2, len(value)), upper):
                    value[k] = value[k] - (value[p] * u0 + value[p + 1] * u1)
            if p + 2 < tile:
                right = right - (local[p] * solved[p] + local[p + 1] * solved[p + 1])
        rows[own] = jnp.where((lane - start > sublane) & (lane < first + size), 0.0, done)
        if own + 1 < count:
            ahead = columns[1][tile:]
        for k in range(own + 1, count):
            terms = [left * value for left, value in zip(columns[k - own], solved)]
            while len(terms) > 1:
                terms = [x + y for x, y in zip(terms[::2], terms[1::2])]
            rows[k] = cleared[k - own] - terms[0]
    return jnp.concatenate(rows, axis=0)


def inverse_factor(block, panel=64):
    size = block.shape[0]
    done = []
    rest = block
    for first in range(0, size, panel):
        rows = eliminate(rest[:panel], first)
        lane = lax.broadcasted_iota(jnp.int32, rows.shape, 1)
        done.append(jnp.where(lane < first + panel, rows, 0.0))
        if first + panel < size:
            rest = rest[panel:]
            lane = lax.broadcasted_iota(jnp.int32, rest.shape, 1)
            pivots = (lane >= first) & (lane < first + panel)
            change = product(rows, rows, ((0,), (0,)))
            rest = jnp.where(pivots, 0.0, rest) - change[first + panel :]
    return jnp.concatenate(done, axis=0)


def transform_of(packed_ref, total):
    half = LANES
    count = total // half
    ROWS, LAST = ((1,), (0,)), ((1,), (1,))
    gram, at = {}, 0
    for column in range(count):
        for row in range(column, count):
            gram[row, column] = packed_ref[at : at + half, :]
            at += half
    pull = [packed_ref[at + 8 * k : at + 8 * k + 1, :] for k in range(count)]
    diagonal = lax.broadcasted_iota(jnp.int32, (half, half), 0) == lax.broadcasted_iota(
        jnp.int32, (half, half), 1
    )
    identity = jnp.where(diagonal, 1.0, 0.0)
    factor, inverse = {}, {}
    for column in range(count):
        for row in range(column, count):
            left = gram[row, column]
            if row == column:
                left = left + identity
            for k in range(column):
                left = left - product(factor[row, k], factor[column, k], LAST)
            if row == column:
                inverse[row, row] = inverse_factor(left)
            else:
                factor[row, column] = product(left, inverse[column, column], LAST)
    for row in range(count):
        for column in range(row):
            total_term = product(factor[row, column], inverse[column, column], ROWS)
            for k in range(column + 1, row):
                total_term = total_term + product(factor[row, k], inverse[k, column], ROWS)
            inverse[row, column] = -product(inverse[row, row], total_term, ROWS)
    inner = [
        sum(
            jnp.sum(inverse[row, column] * pull[column], axis=1, keepdims=True)
            for column in range(row + 1)
        )
        for row in range(count)
    ]
    weights = [
        sum(
            jnp.sum(inverse[row, column] * inner[row], axis=0, keepdims=True)
            for row in range(column, count)
        )
        for column in range(count)
    ]
    zero = jnp.zeros((half, half), jnp.float32)
    return jnp.concatenate(
        [
            jnp.concatenate(
                [inverse.get((row, column), zero) + weights[column] for column in range(count)],
                axis=1,
            )
            for row in range(count)
        ],
        axis=0,
    )


def transform_kernel(total, packed_ref, out_ref):
    out_ref[...] = transform_of(packed_ref, total)


def update_kernel(dims, sources, transform_ref, *refs):
    clusters, terms, members, cols = dims
    slots = return_slots(clusters)
    out = dict(zip(slots, refs[len(sources) :]))
    total = clusters * members
    own = own_cluster(clusters)
    for (source, part), ref in zip(sources, refs):
        targets = [slot for slot in slots if (source, part) in pieces(slot)]
        transform = jnp.concatenate(
            [
                transform_ref[pl.ds(pl.multiple_of((own ^ slot) * members, members), members), :]
                for slot in targets
            ],
            axis=0,
        )
        updated = short_product(transform, ref[0:total, :], ((1,), (0,))) + ref[total : total + 1, :]
        for place, slot in enumerate(targets):
            held = pieces(slot)
            first = sum(len(term_parts(terms)[k]) for _, k in held[: held.index((source, part))])
            for term in range(len(term_parts(terms)[part])):
                out[slot][first + term] = updated[
                    place * members : (place + 1) * members, term * cols : (term + 1) * cols
                ]


def place_kernel(dims, *refs):
    clusters, fields, block_rows, members, cols, groups = dims
    slots = return_slots(clusters)
    values, (out_ref, placed_ref, sent) = refs[: len(slots)], refs[len(slots) :]
    rows = clusters * block_rows
    own = own_cluster(clusters)
    size = members // groups
    copies = []
    for group in range(groups):
        for slot, ref in zip(slots, values):
            held = 0
            for source, part in pieces(slot):
                first = (own ^ (slot ^ source)) * block_rows
                for term in term_parts(fields * block_rows)[part]:
                    field, row = divmod(term, block_rows)
                    at = group * size * fields * rows + field * rows + row + first
                    placed_ref[pl.ds(at, size, stride=fields * rows), :] = ref[
                        held, group * size : (group + 1) * size, :
                    ]
                    held += 1
        span = pl.ds(group * size * fields * rows, size * fields * rows)
        copies.append(pltpu.make_async_copy(placed_ref.at[span], out_ref.at[span], sent.at[group]))
        copies[-1].start()
    for copy in copies:
        copy.wait()


def place(values, clusters, fields, terms):
    _, members, cols = values[0].shape
    rows = clusters * terms
    groups = members // 8
    spec = pl.BlockSpec(memory_space=pltpu.VMEM)
    return pl.pallas_call(
        functools.partial(
            place_kernel, (clusters, fields, terms // fields, members, cols, groups)
        ),
        out_shape=f32(members * rows, cols),
        in_specs=[spec] * len(values),
        out_specs=pl.BlockSpec(memory_space=pl.ANY),
        scratch_shapes=[
            pltpu.VMEM((members * rows, cols), jnp.float32),
            pltpu.SemaphoreType.DMA((groups,)),
        ],
        compiler_params=pltpu.CompilerParams(vmem_limit_bytes=VMEM_LIMIT),
    )(*values)


def on_device(state, obs_values, obs_precision, obs_index):
    members, fields, rows, cols = state.shape
    clusters = lax.axis_size("group") * lax.axis_size("member")
    terms = fields * (rows // clusters)
    total = clusters * members
    width = terms * cols
    dims = (clusters, terms, members, cols)
    sizes = [len(part) for part in term_parts(terms)]
    arrived = exchange(forecast(state, clusters), slot_order(clusters))
    observed = call(observed_kernel, f32(8, width), 3)(obs_values, obs_precision, obs_index)
    packed, *parts = call(
        functools.partial(gram_kernel, dims),
        [f32(448, LANES)] + [f32(total + 8, size * cols) for size in sizes],
        1 + clusters,
        [pltpu.VMEM((total + 8, width), jnp.float32)],
    )(observed, *arrived)
    packed, held = total_over_devices(packed, parts)
    transform = call(functools.partial(transform_kernel, total), f32(total, total), 1)(packed)
    slots = return_slots(clusters)
    sources = sorted({piece for slot in slots for piece in pieces(slot)})
    updated = call(
        functools.partial(update_kernel, dims, sources),
        [f32(sum(sizes[part] for _, part in pieces(slot)), members, cols) for slot in slots],
        1 + len(sources),
    )(transform, *[held[source] for source in sources])
    returned = exchange(updated, slots)
    return place(returned, clusters, fields, terms).reshape(members, fields, rows, cols)


def solution(mesh):
    blocks = P(("group", "member", "space"), None)
    state = P(("group", "member"), None, "space", None)
    return jax.shard_map(
        on_device,
        mesh=mesh,
        in_specs=(state, blocks, blocks, blocks),
        out_specs=state,
        check_vma=False,
    )
```

```python
import functools
import math

import jax
import jax.numpy as jnp
from jax import lax
from jax.experimental import pallas as pl
from jax.experimental.pallas import tpu as pltpu
from jax.sharding import PartitionSpec as P

STEPS = 2
GRAV = 0.4
DEPTH = 0.4
HALO = (4, 3, 2)
HALO_ROWS = sum(HALO)
LANES = 128
DIRECT = 8
GROUP = 32
VMEM_LIMIT = 40 * 1024 * 1024


def whole(shape, memory_space=pltpu.VMEM):
    return pl.BlockSpec(memory_space=memory_space)


def call(kernel, out_shape, n_in, scratch=(), **kw):
    single = not isinstance(out_shape, (list, tuple))
    n_out = 1 if single else len(out_shape)
    spec = pl.BlockSpec(memory_space=pltpu.VMEM)
    return pl.pallas_call(
        kernel,
        out_shape=out_shape,
        in_specs=[spec] * n_in,
        out_specs=spec if single else [spec] * n_out,
        scratch_shapes=list(scratch),
        compiler_params=pltpu.CompilerParams(vmem_limit_bytes=VMEM_LIMIT),
        **kw,
    )


def f32(*shape):
    return jax.ShapeDtypeStruct(shape, jnp.float32)


def pack_kernel(top_ref, bottom_ref, outer_ref, inner_ref):
    edge = top_ref.shape[2]
    even = lax.rem(lax.axis_index("space"), 2) == 0
    at = 0
    for field, rows in enumerate(HALO):
        for row in range(rows):
            to_prev = top_ref[:, field, row, :]
            to_next = bottom_ref[:, field, edge - rows + row, :]
            outer_ref[at] = jnp.where(even, to_prev, to_next)
            inner_ref[at] = jnp.where(even, to_next, to_prev)
            at += 1


def pack_edges(state):
    members, fields, rows, cols = state.shape
    edge = 8
    last = rows // edge - 1
    block = (members, fields, edge, cols)
    out = f32(HALO_ROWS, members, cols)
    out_spec = pl.BlockSpec((HALO_ROWS, members, cols), lambda i: (0, 0, 0))
    return pl.pallas_call(
        pack_kernel,
        grid=(1,),
        out_shape=[out, out],
        in_specs=[
            pl.BlockSpec(block, lambda i: (0, 0, 0, 0)),
            pl.BlockSpec(block, lambda i: (0, 0, last, 0)),
        ],
        out_specs=[out_spec, out_spec],
        compiler_params=pltpu.CompilerParams(vmem_limit_bytes=VMEM_LIMIT),
    )(state, state)


def sweep(first, last, rows, cols, load, store, inside):
    def across_y(value):
        return pltpu.roll(value, cols - 1, 1) - pltpu.roll(value, 1, 1)

    height, height_1 = {}, {}
    flow_x1, flow_y1, flow_x2, flow_y2 = {}, {}, {}, {}
    height[first - 4] = load(0, first - 4)
    height[first - 3] = load(0, first - 3)
    for lead in range(first - 3, last + 7):
        row = lead
        if row < last + 3:
            height[row + 1] = load(0, row + 1)
            flow_x1[row] = inside(
                load(1, row) - GRAV * (height[row + 1] - height[row - 1]), row
            )
            if first - 2 <= row < last + 2:
                flow_y1[row] = load(2, row) - GRAV * across_y(height[row])
        row = lead - 1
        if first - 2 <= row < last + 2:
            height_1[row] = inside(
                height[row]
                - DEPTH * (flow_x1[row + 1] - flow_x1[row - 1] + across_y(flow_y1[row])),
                row,
            )
        row = lead - 2
        if first - 1 <= row < last + 1:
            flow_x2[row] = inside(
                flow_x1[row] - GRAV * (height_1[row + 1] - height_1[row - 1]), row
            )
            if first <= row < last:
                flow_y2[row] = flow_y1[row] - GRAV * across_y(height_1[row])
                store(1, row, flow_x2[row])
                store(2, row, flow_y2[row])
        row = lead - 3
        if first <= row < last:
            store(
                0,
                row,
                height_1[row]
                - DEPTH * (flow_x2[row + 1] - flow_x2[row - 1] + across_y(flow_y2[row])),
            )


def interior_kernel(dims, state_ref, out_ref):
    members, fields, rows, cols, block_rows, edge = dims
    group = min(members, GROUP)
    for at in range(0, members, group):

        def load(field, row):
            start = (at * fields + field) * rows + row
            return state_ref[pl.ds(start, group, stride=fields * rows), :]

        def store(field, row, value):
            block, within = divmod(row, block_rows)
            out_ref[block, field * block_rows + within, at : at + group, :] = value

        sweep(edge, rows - edge, rows, cols, load, store, lambda value, row: value)


def own_cluster(clusters):
    if clusters > DIRECT:
        return 0
    return lax.axis_index("group") * lax.axis_size("member") + lax.axis_index("member")


def edge_kernel(dims, state_ref, outer_ref, inner_ref, interior_ref, *refs):
    members, fields, rows, cols, block_rows, edge = dims
    group = min(members, GROUP)
    clusters = rows // block_rows
    slots, edges_ref = refs[:clusters], refs[clusters]
    here = lax.axis_index("space")
    even = lax.rem(here, 2) == 0
    has_before = (here > 0).astype(jnp.float32)
    has_after = (here < lax.axis_size("space") - 1).astype(jnp.float32)
    own = own_cluster(clusters)

    def inside(value, row):
        if row < 0:
            return value * has_before
        if row >= rows:
            return value * has_after
        return value

    for at in range(0, members, group):

        def load(field, row):
            offset = sum(HALO[:field])
            if row < 0:
                held = offset + HALO[field] + row
                outer, inner = outer_ref[held, at : at + group, :], inner_ref[held, at : at + group, :]
                return jnp.where(even, outer, inner)
            if row >= rows:
                held = offset + row - rows
                outer, inner = outer_ref[held, at : at + group, :], inner_ref[held, at : at + group, :]
                return jnp.where(even, inner, outer)
            start = (at * fields + field) * rows + row
            return state_ref[pl.ds(start, group, stride=fields * rows), :]

        def store(field, row, value):
            block, within = divmod(row, block_rows)
            edges_ref[block, field * block_rows + within, at : at + group, :] = value

        sweep(0, edge, rows, cols, load, store, inside)
        sweep(rows - edge, rows, rows, cols, load, store, inside)
    edges_ref[edge // block_rows : clusters - edge // block_rows] = interior_ref[
        edge // block_rows : clusters - edge // block_rows
    ]
    for slot, ref in zip(slot_order(clusters), slots):
        ref[...] = edges_ref[own ^ slot]


def forecast(state, clusters):
    members, fields, rows, cols = state.shape
    block_rows = rows // clusters
    terms = fields * block_rows
    edge = -(-4 // block_rows) * block_rows
    outer, inner = pack_edges(state)
    count = lax.axis_size("space")

    def trade(value, first):
        pairs = [(i, i + 1) for i in range(first, count - 1, 2)]
        return lax.ppermute(value, "space", pairs + [(j, i) for i, j in pairs])

    outer, inner = trade(outer, 1), trade(inner, 0)
    dims = (members, fields, rows, cols, block_rows, edge)
    flat = state.reshape(members * fields * rows, cols)
    size = members * fields * rows * cols
    interior = call(
        functools.partial(interior_kernel, dims),
        f32(clusters, terms, members, cols),
        1,
        cost_estimate=pl.CostEstimate(
            flops=200 * size, bytes_accessed=16 * size, transcendentals=0
        ),
    )(flat)
    return call(
        functools.partial(edge_kernel, dims),
        [f32(terms, members, cols)] * clusters,
        4,
        [pltpu.VMEM((clusters, terms, members, cols), jnp.float32)],
    )(flat, outer, inner, interior)


def slot_order(clusters):
    if clusters > DIRECT:
        return list(range(clusters))
    cores = lax.axis_size("member")
    return [0] + sorted(range(1, clusters), key=lambda s: (s < cores, s % cores, s))


def exchange(values, slots):
    clusters = lax.axis_size("group") * lax.axis_size("member")
    if clusters > DIRECT:
        stacked = jnp.stack(values, axis=0)
        got = lax.all_to_all(stacked, ("group", "member"), split_axis=0, concat_axis=0, tiled=True)
        return [got[k] for k in range(clusters)]
    return [
        lax.ppermute(value, ("group", "member"), [(i, i ^ slot) for i in range(clusters)])
        if slot
        else value
        for slot, value in zip(slots, values)
    ]


def shares():
    return (lax.axis_size("group"), lax.axis_size("member")) == (4, 2)


def term_parts(terms):
    cuts = [0, terms // 3, terms // 2, terms // 2 + terms // 3, terms] if shares() else [0, terms]
    return [range(first, last) for first, last in zip(cuts, cuts[1:])]


def pieces(slot):
    if not shares():
        return [(0, 0)]
    first, second = 2, 4
    along_first = [(0, 2), (0, 3), (second, 2), (second, 3)]
    along_second = [(0, 0), (0, 1), (first, 0), (first, 1)]
    if slot < first:
        return along_second + along_first
    if slot & first and slot & second:
        return []
    return along_first if slot & first else along_second


def return_slots(clusters):
    return [slot for slot in slot_order(clusters) if pieces(slot)]


def split(value):
    high = value.astype(jnp.bfloat16)
    rest = value - high.astype(jnp.float32)
    middle = rest.astype(jnp.bfloat16)
    low = (rest - middle.astype(jnp.float32)).astype(jnp.bfloat16)
    return high, middle, low


def observed_kernel(values_ref, precision_ref, index_ref, out_ref):
    count = index_ref.shape[1]
    width = out_ref.shape[1]
    parts = list(split(precision_ref[...])) + list(split(values_ref[...]))
    pad = jnp.zeros((16 - len(parts), count), jnp.bfloat16)
    rows = jnp.concatenate(parts + [pad], axis=0)
    position = lax.broadcasted_iota(jnp.int32, (width, count), 0)
    hit = (position == index_ref[...]).astype(jnp.float32).astype(jnp.bfloat16)
    placed = lax.dot_general(
        rows, hit, (((1,), (1,)), ((), ())), preferred_element_type=jnp.float32
    )
    out_ref[0:1, :] = placed[0:1] + placed[1:2] + placed[2:3]
    out_ref[1:2, :] = placed[3:4] + placed[4:5] + placed[5:6]
    out_ref[2:8, :] = jnp.zeros((6, width), jnp.float32)


def product(left, right, contract):
    return lax.dot_general(
        left,
        right,
        (contract, ((), ())),
        precision=lax.Precision.HIGHEST,
        preferred_element_type=jnp.float32,
    )


def gram_kernel(dims, observed_ref, *refs):
    clusters, terms, members, cols = dims
    arrived, (out_ref, *parts, scaled_ref) = refs[:clusters], refs[clusters:]
    total = clusters * members
    scale = 1.0 / math.sqrt(total - 1)
    half = LANES
    own = own_cluster(clusters)
    places = [pl.multiple_of((own ^ slot) * members, members) for slot in slot_order(clusters)]
    for term in range(terms):
        at = slice(term * cols, (term + 1) * cols)
        values = [ref[term] for ref in arrived]
        summed = values[0]
        for value in values[1:]:
            summed = summed + value
        mean = jnp.sum(summed, axis=0, keepdims=True) * (1.0 / total)
        part = [term in held for held in term_parts(terms)].index(True)
        there = term - term_parts(terms)[part].start
        there = slice(there * cols, (there + 1) * cols)
        parts[part][total : total + 8, there] = jnp.broadcast_to(mean, (8, cols))
        weight = observed_ref[0:1, at] * scale
        for place, value in zip(places, values):
            anomaly = value - mean
            parts[part][pl.ds(place, members), there] = anomaly
            scaled_ref[pl.ds(place, members), at] = anomaly * weight
        innovation = (observed_ref[1:2, at] - mean) * weight
        scaled_ref[total : total + 8, at] = jnp.concatenate(
            [innovation, jnp.zeros((7, cols), jnp.float32)], axis=0
        )
    result = short_product(scaled_ref[...], scaled_ref[0:total, :], ((1,), (1,)), low_terms=True)
    at = 0
    for first in range(0, total, half):
        out_ref[at : at + total - first, :] = result[first:total, first : first + half]
        at += total - first
    for k, first in enumerate(range(0, total, half)):
        out_ref[at + 8 * k : at + 8 * k + 8, :] = result[total : total + 8, first : first + half]
    at += 8 * (total // half)
    if at < out_ref.shape[0]:
        out_ref[at:, :] = jnp.zeros((out_ref.shape[0] - at, half), jnp.float32)


def flip(value, axis, bits):
    return lax.ppermute(value, axis, [(i, i ^ bits) for i in range(lax.axis_size(axis))])


def total_over_devices(value, parts):
    held = {(0, k): part for k, part in enumerate(parts)}
    if not shares() or lax.axis_size("space") != 4:
        if shares():
            for k, part in enumerate(parts):
                bit = 1 + k // 2
                held[2 * bit, k] = flip(part, "group", bit)
        return lax.psum(value, ("group", "member", "space")), held
    rows, cols = value.shape
    core = lax.axis_index("member")
    chip = lax.axis_index("group")
    half = rows // 2
    part = half // 4
    kept = lax.dynamic_slice_in_dim(value, core * half, half, 0)
    given = lax.dynamic_slice_in_dim(value, (1 - core) * half, half, 0)
    summed = (kept + flip(given, "member", 1)).reshape(4, part, cols)
    pieces = [lax.dynamic_index_in_dim(summed, chip ^ s, 0, False) for s in range(4)]
    piece = pieces[0] + (
        flip(pieces[1], "group", 1) + flip(pieces[2], "group", 2) + flip(pieces[3], "group", 3)
    )
    piece, early0, early2 = lax.optimization_barrier((piece, parts[0], parts[2]))
    early0, early2 = flip(early0, "group", 1), flip(early2, "group", 2)
    piece = piece + (flip(piece, "space", 3) + flip(piece, "space", 2) + flip(piece, "space", 1))
    piece, held[2, 0], held[4, 2] = lax.optimization_barrier((piece, early0, early2))
    got = jnp.stack([piece] + [flip(piece, "group", s) for s in (1, 2, 3)], axis=0)
    mine = jnp.concatenate(
        [lax.dynamic_index_in_dim(got, chip ^ i, 0, False) for i in range(4)], axis=0
    )
    mine, late1, late3 = lax.optimization_barrier((mine, parts[1], parts[3]))
    held[2, 1], held[4, 3] = flip(late1, "group", 1), flip(late3, "group", 2)
    other = flip(mine, "member", 1)
    whole_sum = jnp.concatenate(
        [jnp.where(core == 0, mine, other), jnp.where(core == 0, other, mine)], axis=0
    )
    return whole_sum, held


def short_product(left, right, contract, low_terms=False):
    left_high, right_high = left.astype(jnp.bfloat16), right.astype(jnp.bfloat16)
    left_low = (left - left_high.astype(jnp.float32)).astype(jnp.bfloat16)
    right_low = (right - right_high.astype(jnp.float32)).astype(jnp.bfloat16)

    def dot(x, y):
        return lax.dot_general(x, y, (contract, ((), ())), preferred_element_type=jnp.float32)

    small = dot(left_high, right_low) + dot(left_low, right_high)
    if low_terms:
        small = small + dot(left_low, right_low)
    return dot(left_high, right_high) + small


def eliminate(panel, first):
    tile = 8
    size, width = panel.shape
    count = size // tile
    rows = [panel[at : at + tile, :] for at in range(0, size, tile)]
    lane = lax.broadcasted_iota(jnp.int32, (tile, width), 1)
    sublane = lax.broadcasted_iota(jnp.int32, (tile, width), 0)

    def row(value, at):
        return jnp.broadcast_to(value[at : at + 1, :], (tile, width))

    def column(value, at):
        return jnp.broadcast_to(value[:, at : at + 1], (tile, width))

    ahead = None
    for own in range(count):
        start = first + own * tile
        columns = [[column(value, start + k) for k in range(tile)] for value in rows[own:]]
        if ahead is not None:
            columns[0] = ahead
        if own + 1 < count:
            for value, spread in zip(rows[own : own + 2], columns):
                spread += [column(value, start + k) for k in range(tile, 2 * tile)]
        pivots = (lane >= start) & (lane < start + tile)
        cleared = [jnp.where(pivots, 0.0, value) for value in rows[own:]]
        local = columns[0]
        right = jnp.where(lane - start == sublane, 1.0, cleared[0])
        done = right
        solved = []
        for p in range(0, tile, 2):
            s00, s10, s11 = row(local[p], p), row(local[p], p + 1), row(local[p + 1], p + 1)
            inv0 = 1.0 / s00
            inv1 = s00 * (1.0 / (s00 * s11 - s10 * s10))
            low = s10 * inv0
            upper = []
            for k in range(p + 2, len(local)):
                u0 = row(local[k], p)
                upper.append((u0 * inv0, (row(local[k], p + 1) - low * u0) * inv1))
            r0 = row(right, p)
            r1 = row(right, p + 1) - low * r0
            solved += [r0 * inv0, r1 * inv1]
            done = jnp.where(sublane == p, r0 * lax.rsqrt(s00), done)
            done = jnp.where(sublane == p + 1, r1 * (inv1 * lax.rsqrt(inv1)), done)
            for value in columns:
                value[p + 1] = value[p + 1] - low * value[p]
                for k, (u0, u1) in zip(range(p + 2, len(value)), upper):
                    value[k] = value[k] - (value[p] * u0 + value[p + 1] * u1)
            if p + 2 < tile:
                right = right - (local[p] * solved[p] + local[p + 1] * solved[p + 1])
        rows[own] = jnp.where((lane - start > sublane) & (lane < first + size), 0.0, done)
        if own + 1 < count:
            ahead = columns[1][tile:]
        for k in range(own + 1, count):
            terms = [left * value for left, value in zip(columns[k - own], solved)]
            while len(terms) > 1:
                terms = [x + y for x, y in zip(terms[::2], terms[1::2])]
            rows[k] = cleared[k - own] - terms[0]
    return jnp.concatenate(rows, axis=0)


def inverse_factor(block, panel=64):
    size = block.shape[0]
    done = []
    rest = block
    for first in range(0, size, panel):
        rows = eliminate(rest[:panel], first)
        lane = lax.broadcasted_iota(jnp.int32, rows.shape, 1)
        done.append(jnp.where(lane < first + panel, rows, 0.0))
        if first + panel < size:
            rest = rest[panel:]
            lane = lax.broadcasted_iota(jnp.int32, rest.shape, 1)
            pivots = (lane >= first) & (lane < first + panel)
            change = product(rows, rows, ((0,), (0,)))
            rest = jnp.where(pivots, 0.0, rest) - change[first + panel :]
    return jnp.concatenate(done, axis=0)


def transform_of(packed_ref, total):
    half = LANES
    count = total // half
    ROWS, LAST = ((1,), (0,)), ((1,), (1,))
    gram, at = {}, 0
    for column in range(count):
        for row in range(column, count):
            gram[row, column] = packed_ref[at : at + half, :]
            at += half
    pull = [packed_ref[at + 8 * k : at + 8 * k + 1, :] for k in range(count)]
    diagonal = lax.broadcasted_iota(jnp.int32, (half, half), 0) == lax.broadcasted_iota(
        jnp.int32, (half, half), 1
    )
    identity = jnp.where(diagonal, 1.0, 0.0)
    factor, inverse = {}, {}
    for column in range(count):
        for row in range(column, count):
            left = gram[row, column]
            if row == column:
                left = left + identity
            for k in range(column):
                left = left - product(factor[row, k], factor[column, k], LAST)
            if row == column:
                inverse[row, row] = inverse_factor(left)
            else:
                factor[row, column] = product(left, inverse[column, column], LAST)
    for row in range(count):
        for column in range(row):
            total_term = short_product(factor[row, column], inverse[column, column], ROWS)
            for k in range(column + 1, row):
                total_term = total_term + short_product(factor[row, k], inverse[k, column], ROWS)
            inverse[row, column] = -short_product(inverse[row, row], total_term, ROWS)
    inner = [
        sum(
            jnp.sum(inverse[row, column] * pull[column], axis=1, keepdims=True)
            for column in range(row + 1)
        )
        for row in range(count)
    ]
    weights = [
        sum(
            jnp.sum(inverse[row, column] * inner[row], axis=0, keepdims=True)
            for row in range(column, count)
        )
        for column in range(count)
    ]
    zero = jnp.zeros((half, half), jnp.float32)
    return jnp.concatenate(
        [
            jnp.concatenate(
                [inverse.get((row, column), zero) + weights[column] for column in range(count)],
                axis=1,
            )
            for row in range(count)
        ],
        axis=0,
    )


def transform_kernel(total, packed_ref, out_ref):
    out_ref[...] = transform_of(packed_ref, total)


def update_kernel(dims, sources, transform_ref, *refs):
    clusters, terms, members, cols = dims
    slots = return_slots(clusters)
    out = dict(zip(slots, refs[len(sources) :]))
    total = clusters * members
    own = own_cluster(clusters)
    for (source, part), ref in zip(sources, refs):
        targets = [slot for slot in slots if (source, part) in pieces(slot)]
        transform = jnp.concatenate(
            [
                transform_ref[pl.ds(pl.multiple_of((own ^ slot) * members, members), members), :]
                for slot in targets
            ],
            axis=0,
        )
        updated = short_product(transform, ref[0:total, :], ((1,), (0,))) + ref[total : total + 1, :]
        for place, slot in enumerate(targets):
            held = pieces(slot)
            first = sum(len(term_parts(terms)[k]) for _, k in held[: held.index((source, part))])
            for term in range(len(term_parts(terms)[part])):
                out[slot][first + term] = updated[
                    place * members : (place + 1) * members, term * cols : (term + 1) * cols
                ]


def place_kernel(dims, *refs):
    clusters, fields, block_rows, members, cols, groups = dims
    slots = return_slots(clusters)
    values, (out_ref, placed_ref, sent) = refs[: len(slots)], refs[len(slots) :]
    rows = clusters * block_rows
    own = own_cluster(clusters)
    size = members // groups
    copies = []
    for group in range(groups):
        for slot, ref in zip(slots, values):
            held = 0
            for source, part in pieces(slot):
                first = (own ^ (slot ^ source)) * block_rows
                for term in term_parts(fields * block_rows)[part]:
                    field, row = divmod(term, block_rows)
                    at = group * size * fields * rows + field * rows + row + first
                    placed_ref[pl.ds(at, size, stride=fields * rows), :] = ref[
                        held, group * size : (group + 1) * size, :
                    ]
                    held += 1
        span = pl.ds(group * size * fields * rows, size * fields * rows)
        copies.append(pltpu.make_async_copy(placed_ref.at[span], out_ref.at[span], sent.at[group]))
        copies[-1].start()
    for copy in copies:
        copy.wait()


def place(values, clusters, fields, terms):
    _, members, cols = values[0].shape
    rows = clusters * terms
    groups = members // 8
    spec = pl.BlockSpec(memory_space=pltpu.VMEM)
    return pl.pallas_call(
        functools.partial(
            place_kernel, (clusters, fields, terms // fields, members, cols, groups)
        ),
        out_shape=f32(members * rows, cols),
        in_specs=[spec] * len(values),
        out_specs=pl.BlockSpec(memory_space=pl.ANY),
        scratch_shapes=[
            pltpu.VMEM((members * rows, cols), jnp.float32),
            pltpu.SemaphoreType.DMA((groups,)),
        ],
        compiler_params=pltpu.CompilerParams(vmem_limit_bytes=VMEM_LIMIT),
    )(*values)


def on_device(state, obs_values, obs_precision, obs_index):
    members, fields, rows, cols = state.shape
    clusters = lax.axis_size("group") * lax.axis_size("member")
    terms = fields * (rows // clusters)
    total = clusters * members
    width = terms * cols
    dims = (clusters, terms, members, cols)
    sizes = [len(part) for part in term_parts(terms)]
    arrived = exchange(forecast(state, clusters), slot_order(clusters))
    observed = call(observed_kernel, f32(8, width), 3)(obs_values, obs_precision, obs_index)
    packed, *parts = call(
        functools.partial(gram_kernel, dims),
        [f32(448, LANES)] + [f32(total + 8, size * cols) for size in sizes],
        1 + clusters,
        [pltpu.VMEM((total + 8, width), jnp.float32)],
    )(observed, *arrived)
    packed, held = total_over_devices(packed, parts)
    transform = call(functools.partial(transform_kernel, total), f32(total, total), 1)(packed)
    slots = return_slots(clusters)
    sources = sorted({piece for slot in slots for piece in pieces(slot)})
    updated = call(
        functools.partial(update_kernel, dims, sources),
        [f32(sum(sizes[part] for _, part in pieces(slot)), members, cols) for slot in slots],
        1 + len(sources),
    )(transform, *[held[source] for source in sources])
    returned = exchange(updated, slots)
    return place(returned, clusters, fields, terms).reshape(members, fields, rows, cols)


def solution(mesh):
    blocks = P(("group", "member", "space"), None)
    state = P(("group", "member"), None, "space", None)
    return jax.shard_map(
        on_device,
        mesh=mesh,
        in_specs=(state, blocks, blocks, blocks),
        out_specs=state,
        check_vma=False,
    )
```
